128 devices in a mesh: row: 4 (over x_lo, core), col: 8 (over x_hi, y), depth: 4 (over z).
Axes of the slice: x: 4 (x_hi: 2, x_lo: 2; x = x_hi * 2 + x_lo), y: 4, z: 4, core: 2. Of those that a mesh axis runs over, the one named last changes fastest.
Arguments:
- tokens: bfloat16 [1024, 12288], P(('row', 'col'), 'depth'), may hold values from -6 to 6
- w_qkv: bfloat16 [12288, 64, 3, 128], P('depth', ('row', 'col')), may hold values from -0.0546875 to 0.0546875
- w_out: bfloat16 [64, 128, 12288], P(('row', 'col'), None, 'depth'), may hold values from -0.125 to 0.125
- positions: int32 [1024], P('depth'), may hold values from 0 to 255, as said below
- d_output: bfloat16 [1024, 12288], P(('row', 'col'), 'depth'), may hold values from -1.5 to 1.5
Outputs:
- output: bfloat16 [1024, 12288], P(('row', 'col'), 'depth')
- d_tokens: bfloat16 [1024, 12288], P(('row', 'col'), 'depth')
- d_qkv_weight: float32 [12288, 64, 3, 128], P('depth', ('row', 'col'))
- d_out_weight: float32 [64, 128, 12288], P(('row', 'col'), None, 'depth')
The draws below stay inside these ranges and needn't reach their ends.
Inputs may be any that keep to these rules, and one draw needn't show every extreme that they name: Within each sequence of 256 tokens the positions start at 0 on its first token and either rise by one from token to token or fall back to 0 where a new document begins; in some sequence one document fills all 256 tokens.
All inputs are finite; a program needn't handle non-finite values.
Results may differ from the reference program's by a relative error of at most 0.03.
Values may be sent and summed in bfloat16 or wider, within the bound.
No kernel may reach another device: no remote copies, remote signals or barrier semaphores. Data moves between devices by JAX's collectives and lax.ppermute only.
A program may use at most 128 MiB of HBM per device.

```python
import math
import jax
import jax.numpy as jnp
from jax import lax

D = 12288
HEADS = 64
HEAD = 128
SEQ = 256
TOKENS = 1024
N_ROW = 4
N_COL = 8


def draw_positions(key, part):
    key = jax.random.fold_in(key, 7)
    first_key, second_key = jax.random.split(key)
    sequences = TOKENS // SEQ
    boundary = jax.random.randint(first_key, (sequences, SEQ), 0, SEQ) < 3
    places = jnp.arange(SEQ, dtype=jnp.int32)[None, :]
    whole_seq = jax.random.randint(second_key, (), 0, sequences)
    rows_index = jnp.arange(sequences, dtype=jnp.int32)[:, None]
    boundary = jnp.where((rows_index == whole_seq) & (places > 0), False, boundary)
    boundary = jnp.where(places == 0, True, boundary)
    starts = jnp.where(boundary, places, 0)
    latest = lax.cummax(starts, axis=1)
    return (places - latest).reshape(TOKENS).astype(jnp.int32)


def block_scale(own_key, dims, pieces, low, top_value):
    loudness = 1.0
    for axis_at, parts in pieces:
        steps = jax.random.uniform(jax.random.fold_in(jax.random.fold_in(own_key, 6), axis_at), (parts,), jnp.float32, low / len(pieces), top_value / len(pieces))
        loudness = loudness * jnp.repeat(jnp.exp(steps), dims[axis_at] // parts).reshape((-1,) + (1,) * (len(dims) - 1 - axis_at))
    return loudness


def centred(key, dims, width, limit, shards=(), kind=jnp.bfloat16):
    level = block_scale(key, dims, shards, -0.22, 0.18) if shards else 1.0
    values = jax.random.normal(key, dims, jnp.float32) * width * level
    return jnp.minimum(jnp.maximum(values, -limit), limit).astype(kind)


def setup_inputs(seed: int = 0) -> dict:
    seeds = jax.random.split(jax.random.key(seed), 6)
    tokens = centred(seeds[0], (TOKENS, D), 1.0, 6.0, ((0, 32), (1, 4)))
    w_qkv = centred(seeds[1], (D, HEADS, 3, HEAD), D ** -0.5, 0.0546875, ((0, 4), (1, 32)))
    w_out = centred(seeds[2], (HEADS, HEAD, D), (HEADS * HEAD // 4) ** -0.5, 0.125, ((0, 32), (2, 4)))
    positions = draw_positions(jax.random.fold_in(seeds[5], 71), 0)
    d_output = centred(seeds[4], (TOKENS, D), 0.25, 1.5, ((0, 32), (1, 4)))
    return {"tokens": tokens, "w_qkv": w_qkv, "w_out": w_out, "positions": positions, "d_output": d_output}


def allowed_pairs(seq_positions):
    places = jnp.arange(seq_positions.shape[0], dtype=jnp.int32)
    earlier = places[None, :] <= places[:, None]
    inside = places[None, :] >= (places - seq_positions)[:, None]
    return earlier & inside

def forward_sequence(projected_seq, seq_positions):
    score_scale = 1.0 / math.sqrt(HEAD)
    queries = projected_seq[:, :, 0].astype(jnp.float32)
    key_rows = projected_seq[:, :, 1].astype(jnp.float32)
    value_rows = projected_seq[:, :, 2].astype(jnp.float32)
    allowed = allowed_pairs(seq_positions)
    scores = jnp.einsum('ihd,jhd->hij', queries, key_rows) * score_scale
    weights = jnp.where(allowed[None], jnp.exp(scores), jnp.float32(0.0))
    probabilities = weights / lax.optimization_barrier(jnp.sum(weights, axis=-1, keepdims=True))
    rounded = probabilities.astype(jnp.bfloat16)
    mixed_heads = jnp.einsum('hij,jhd->ihd', rounded.astype(jnp.float32), value_rows).astype(jnp.bfloat16)
    return (mixed_heads, probabilities, rounded)

def backward_sequence(projected_seq, probabilities, rounded, d_mixed):
    score_scale = 1.0 / math.sqrt(HEAD)
    queries = projected_seq[:, :, 0].astype(jnp.float32)
    key_rows = projected_seq[:, :, 1].astype(jnp.float32)
    value_rows = projected_seq[:, :, 2].astype(jnp.float32)
    grad_mixed = d_mixed.astype(jnp.float32)
    d_probs = jnp.einsum('ihd,jhd->hij', grad_mixed, value_rows)
    row_delta = lax.optimization_barrier(jnp.sum(probabilities * d_probs, axis=-1, keepdims=True))
    d_scores = (probabilities * (d_probs - row_delta) * score_scale).astype(jnp.bfloat16).astype(jnp.float32)
    grad_query = jnp.einsum('hij,jhd->ihd', d_scores, key_rows)
    grad_key = jnp.einsum('hij,ihd->jhd', d_scores, queries)
    grad_value = jnp.einsum('hij,ihd->jhd', rounded.astype(jnp.float32), grad_mixed)
    return jnp.stack([grad_query, grad_key, grad_value], axis=2).astype(jnp.bfloat16)

def grouped_sum(left, right, head_groups):
    group_width = left.shape[1] // head_groups
    lefts = left.reshape(left.shape[0], head_groups, group_width).transpose(1, 0, 2)
    rights = right.reshape(head_groups, group_width, right.shape[1])

    def add_group(running, operands):
        term = jnp.dot(operands[0], operands[1], preferred_element_type=jnp.float32).astype(jnp.bfloat16)
        term = lax.optimization_barrier(term)
        return (running + term.astype(jnp.float32), None)
    start_sum = jnp.zeros((left.shape[0], right.shape[1]), jnp.float32)
    running, _ = lax.scan(add_group, start_sum, (lefts, rights))
    return running

def reference(tokens, w_qkv, w_out, positions, d_output):
    sequences = tokens.shape[0] // SEQ
    hidden = HEADS * HEAD
    head_groups = N_ROW * N_COL
    qkv_flat = w_qkv.reshape(D, HEADS * 3 * HEAD)
    out_flat = w_out.reshape(hidden, D)
    projected = jnp.dot(tokens, qkv_flat, preferred_element_type=jnp.float32).astype(jnp.bfloat16)
    projected = projected.reshape(sequences, SEQ, HEADS, 3, HEAD)
    seq_positions = positions.reshape(sequences, SEQ)
    mixed_heads, probabilities, rounded = jax.vmap(forward_sequence)(projected, seq_positions)
    mixed_flat = mixed_heads.reshape(TOKENS, hidden)
    output = grouped_sum(mixed_flat, out_flat, head_groups).astype(jnp.bfloat16)
    d_mixed = jnp.dot(d_output, out_flat.T, preferred_element_type=jnp.float32).astype(jnp.bfloat16)
    d_out_weight = jnp.dot(mixed_flat.T, d_output, preferred_element_type=jnp.float32).reshape(HEADS, HEAD, D)
    d_projected = jax.vmap(backward_sequence)(projected, probabilities, rounded, d_mixed.reshape(sequences, SEQ, HEADS, HEAD))
    d_projected = d_projected.reshape(TOKENS, HEADS * 3 * HEAD)
    d_qkv_weight = jnp.dot(tokens.T, d_projected, preferred_element_type=jnp.float32).reshape(D, HEADS, 3, HEAD)
    d_tokens = grouped_sum(d_projected, qkv_flat.T, head_groups).astype(jnp.bfloat16)
    return (output, d_tokens, d_qkv_weight, d_out_weight)
```

```python
import math

import jax
import jax.numpy as jnp
from jax import lax
from jax.experimental import pallas as pl
from jax.experimental.pallas import tpu as pltpu
from jax.sharding import PartitionSpec as P

PLANE = ("row", "col")
BLOCK = 32
BLOCKS = 32
OFFSETS = (1, 3, 2)


def plane_index(x, y, core):
    return ((x % 2) * 2 + core) * 8 + (x // 2) * 4 + y


def ring_pairs(offset, first):
    pairs = []
    for x in range(4):
        for y in range(4):
            for core in range(2):
                along_x = (core == 0) == first
                sx, sy = ((x + offset) % 4, y) if along_x else (x, (y + offset) % 4)
                pairs.append((plane_index(sx, sy, core), plane_index(x, y, core)))
    return pairs


def core_pairs():
    return [
        (plane_index(x, y, core), plane_index(x, y, 1 - core))
        for x in range(4)
        for y in range(4)
        for core in range(2)
    ]


def depth_pairs(offset):
    return [((z + offset) % 4, z) for z in range(4)]


def swap_cores(rows):
    return lax.ppermute(rows, PLANE, core_pairs())


def from_ring(rows, offset, first):
    return lax.ppermute(rows, PLANE, ring_pairs(offset, first))


def from_depth(rows, offset):
    return lax.ppermute(rows, "depth", depth_pairs(offset))


def block_tables(depth):
    row, col = lax.axis_index("row"), lax.axis_index("col")
    x, y, core = (col // 4) * 2 + row // 2, col % 4, row % 2
    place = jnp.arange(BLOCKS, dtype=jnp.int32)
    j, family, i = place // 8, (place // 4) % 2, place % 4
    of_core = (core + family) % 2
    dx, dy = jnp.where(of_core == 0, i, j), jnp.where(of_core == 0, j, i)
    sx, sy = (x + dx) % 4, (y + dy) % 4
    sequence = (sx % 2) * 2 + of_core
    forward = ((sequence - depth + 4) % 4) * 8 + (sx // 2) * 4 + sy
    sequence = (place // 8 + depth) % 4
    of_core = sequence % 2
    sx, sy = ((place % 8) // 4) * 2 + sequence // 2, place % 4
    family = (of_core + core) % 2
    dx, dy = (sx - x + 4) % 4, (sy - y + 4) % 4
    i, j = jnp.where(of_core == 0, dx, dy), jnp.where(of_core == 0, dy, dx)
    inverse = j * 8 + family * 4 + i
    return forward.astype(jnp.int32), inverse.astype(jnp.int32)


def place_blocks(parts, table):
    columns = parts[0].shape[-1]
    per_part = parts[0].shape[0] // BLOCK
    parts = [part.reshape(per_part, BLOCK, columns) for part in parts]

    def kernel(table_ref, *refs):
        out_ref = refs[-1]
        for at, ref in enumerate(refs[:-1]):
            for b in range(per_part):
                out_ref[table_ref[at * per_part + b]] = ref[b]

    placed = pl.pallas_call(
        kernel,
        out_shape=jax.ShapeDtypeStruct((BLOCKS, BLOCK, columns), parts[0].dtype),
        in_specs=[pl.BlockSpec(memory_space=pltpu.SMEM)]
        + [pl.BlockSpec(memory_space=pltpu.VMEM)] * len(parts),
        out_specs=pl.BlockSpec(memory_space=pltpu.VMEM),
        compiler_params=pltpu.CompilerParams(vmem_limit_bytes=24 * 2**20),
    )(table, *parts)
    return placed.reshape(BLOCKS * BLOCK, columns)


def allowed_pairs(seq_positions):
    places = jnp.arange(seq_positions.shape[0], dtype=jnp.int32)
    earlier = places[None, :] <= places[:, None]
    inside = places[None, :] >= (places - seq_positions)[:, None]
    return earlier & inside


def attend(queries, key_rows, value_rows, allowed, score_scale):
    scores = (
        jnp.einsum("ihd,jhd->hij", queries, key_rows, preferred_element_type=jnp.float32)
        * score_scale
    )
    weights = jnp.where(allowed[None], jnp.exp(scores), 0.0)
    probabilities = weights / jnp.sum(weights, axis=-1, keepdims=True)
    rounded = probabilities.astype(jnp.bfloat16)
    mixed_heads = jnp.einsum(
        "hij,jhd->ihd", rounded, value_rows, preferred_element_type=jnp.float32
    ).astype(jnp.bfloat16)
    return (mixed_heads, probabilities, rounded)


def attend_back(queries, key_rows, value_rows, probabilities, rounded, d_mixed, score_scale):
    d_probs = jnp.einsum("ihd,jhd->hij", d_mixed, value_rows, preferred_element_type=jnp.float32)
    row_delta = jnp.sum(probabilities * d_probs, axis=-1, keepdims=True)
    d_scores = (probabilities * (d_probs - row_delta) * score_scale).astype(jnp.bfloat16)
    grad_query = jnp.einsum("hij,jhd->ihd", d_scores, key_rows, preferred_element_type=jnp.float32)
    grad_key = jnp.einsum("hij,ihd->jhd", d_scores, queries, preferred_element_type=jnp.float32)
    grad_value = jnp.einsum("hij,ihd->jhd", rounded, d_mixed, preferred_element_type=jnp.float32)
    return jnp.stack([grad_query, grad_key, grad_value], axis=2).astype(jnp.bfloat16)


def gather_second(column):
    chunks = [None] * 4
    for j in (0,) + OFFSETS:
        own = column if j == 0 else from_ring(column, j, False)
        chunks[j] = jnp.concatenate([own, swap_cores(own)], axis=0)
    return chunks


def sum_float32(parts):
    total = parts[0].astype(jnp.float32)
    for part in parts[1:]:
        total = total + part.astype(jnp.float32)
    return total


def scatter_plane(terms):
    half = 4 * BLOCK
    pieces = [None] * 4
    for j in (2, 1, 3, 0):
        other = swap_cores(terms[j][half:])
        pair = sum_float32([terms[j][:half], other]).astype(jnp.bfloat16)
        pieces[j] = pair if j == 0 else from_ring(pair, 4 - j, False)
    column = sum_float32(pieces).astype(jnp.bfloat16).reshape(4, BLOCK, -1)
    parts = [column[0]] + [from_ring(column[i], 4 - i, True) for i in (2, 1, 3)]
    return sum_float32(parts).astype(jnp.bfloat16)


def scatter_depth(rows, seq_len):
    parts = [rows[:seq_len]]
    for k in (2, 1, 3):
        parts.append(from_depth(rows[k * seq_len : (k + 1) * seq_len], 4 - k))
    return sum_float32(parts).astype(jnp.bfloat16)


def gather_depth(rows):
    ahead = {k: from_depth(rows, k) for k in (2, 1, 3)}
    return [rows, ahead[1], ahead[2], ahead[3]]


def per_device(tokens, w_qkv, w_out, positions, d_output):
    seq_len = positions.shape[0]
    local_heads = w_qkv.shape[1]
    head_size = w_qkv.shape[3]
    width_part = w_qkv.shape[0]
    score_scale = 1.0 / math.sqrt(head_size)
    qkv_flat = w_qkv.reshape(width_part, local_heads * 3 * head_size)
    out_flat = w_out.reshape(local_heads * head_size, width_part)
    contract_first = (((0,), (0,)), ((), ()))
    contract_last = (((1,), (1,)), ((), ()))
    depth = lax.axis_index("depth")
    forward, inverse = block_tables(depth)

    both = jnp.concatenate([tokens, d_output], axis=1)
    near = {i: from_ring(both, i, True) for i in OFFSETS}
    near[0] = both
    column = jnp.concatenate([near[i] for i in range(4)], axis=0)

    token_chunks = gather_second(column[:, :width_part])
    projected = place_blocks(
        [
            jnp.dot(chunk, qkv_flat, preferred_element_type=jnp.float32).astype(jnp.bfloat16)
            for chunk in token_chunks
        ],
        forward,
    )
    projected = scatter_depth(projected, seq_len)
    projected = projected.reshape(seq_len, local_heads, 3, head_size)
    queries = projected[:, :, 0]
    key_rows = projected[:, :, 1]
    value_rows = projected[:, :, 2]
    allowed = allowed_pairs(positions)
    mixed_heads, probabilities, rounded = attend(
        queries, key_rows, value_rows, allowed, score_scale
    )
    heads_all = place_blocks(
        gather_depth(mixed_heads.reshape(seq_len, local_heads * head_size)), inverse
    )
    rows = 8 * BLOCK
    output = scatter_plane(
        [
            jnp.dot(
                heads_all[j * rows : (j + 1) * rows], out_flat, preferred_element_type=jnp.float32
            ).astype(jnp.bfloat16)
            for j in range(4)
        ]
    )

    grad_chunks = gather_second(column[:, width_part:])
    d_mixed = place_blocks(
        [
            lax.dot_general(
                chunk, out_flat, contract_last, preferred_element_type=jnp.float32
            ).astype(jnp.bfloat16)
            for chunk in grad_chunks
        ],
        forward,
    )
    d_mixed = scatter_depth(d_mixed, seq_len).reshape(seq_len, local_heads, head_size)
    d_projected = attend_back(
        queries, key_rows, value_rows, probabilities, rounded, d_mixed, score_scale
    )
    projected_grads = place_blocks(
        gather_depth(d_projected.reshape(seq_len, local_heads * 3 * head_size)), inverse
    )
    d_tokens = scatter_plane(
        [
            lax.dot_general(
                projected_grads[j * rows : (j + 1) * rows],
                qkv_flat,
                contract_last,
                preferred_element_type=jnp.float32,
            ).astype(jnp.bfloat16)
            for j in range(4)
        ]
    )
    d_out_weight = lax.dot_general(
        heads_all,
        jnp.concatenate(grad_chunks, axis=0),
        contract_first,
        preferred_element_type=jnp.float32,
    )
    d_out_weight = d_out_weight.reshape(local_heads, head_size, width_part)
    d_qkv_weight = lax.dot_general(
        jnp.concatenate(token_chunks, axis=0),
        projected_grads,
        contract_first,
        preferred_element_type=jnp.float32,
    )
    d_qkv_weight = d_qkv_weight.reshape(width_part, local_heads, 3, head_size)
    return (output, d_tokens, d_qkv_weight, d_out_weight)


def solution(mesh):
    in_specs = (
        P(("row", "col"), "depth"),
        P("depth", ("row", "col"), None, None),
        P(("row", "col"), None, "depth"),
        P("depth"),
        P(("row", "col"), "depth"),
    )
    out_specs = (
        P(("row", "col"), "depth"),
        P(("row", "col"), "depth"),
        P("depth", ("row", "col"), None, None),
        P(("row", "col"), None, "depth"),
    )
    return jax.shard_map(
        per_device, mesh=mesh, in_specs=in_specs, out_specs=out_specs, check_vma=False
    )
```

```python
import math

import jax
import jax.numpy as jnp
from jax import lax
from jax.experimental import pallas as pl
from jax.experimental.pallas import tpu as pltpu
from jax.sharding import PartitionSpec as P

PLANE = ("row", "col")
BLOCK = 32
BLOCKS = 32
OFFSETS = (1, 3, 2)


def plane_index(x, y, core):
    return ((x % 2) * 2 + core) * 8 + (x // 2) * 4 + y


def ring_pairs(offset, first):
    pairs = []
    for x in range(4):
        for y in range(4):
            for core in range(2):
                along_x = (core == 0) == first
                sx, sy = ((x + offset) % 4, y) if along_x else (x, (y + offset) % 4)
                pairs.append((plane_index(sx, sy, core), plane_index(x, y, core)))
    return pairs


def core_pairs():
    return [
        (plane_index(x, y, core), plane_index(x, y, 1 - core))
        for x in range(4)
        for y in range(4)
        for core in range(2)
    ]


def depth_pairs(offset):
    return [((z + offset) % 4, z) for z in range(4)]


def swap_cores(rows):
    return lax.ppermute(rows, PLANE, core_pairs())


def from_ring(rows, offset, first):
    return lax.ppermute(rows, PLANE, ring_pairs(offset, first))


def from_depth(rows, offset):
    return lax.ppermute(rows, "depth", depth_pairs(offset))


def block_tables(depth):
    row, col = lax.axis_index("row"), lax.axis_index("col")
    x, y, core = (col // 4) * 2 + row // 2, col % 4, row % 2
    place = jnp.arange(BLOCKS, dtype=jnp.int32)
    j, family, i = place // 8, (place // 4) % 2, place % 4
    of_core = (core + family) % 2
    dx, dy = jnp.where(of_core == 0, i, j), jnp.where(of_core == 0, j, i)
    sx, sy = (x + dx) % 4, (y + dy) % 4
    sequence = (sx % 2) * 2 + of_core
    forward = ((sequence - depth + 4) % 4) * 8 + (sx // 2) * 4 + sy
    sequence = (place // 8 + depth) % 4
    of_core = sequence % 2
    sx, sy = ((place % 8) // 4) * 2 + sequence // 2, place % 4
    family = (of_core + core) % 2
    dx, dy = (sx - x + 4) % 4, (sy - y + 4) % 4
    i, j = jnp.where(of_core == 0, dx, dy), jnp.where(of_core == 0, dy, dx)
    inverse = j * 8 + family * 4 + i
    return forward.astype(jnp.int32), inverse.astype(jnp.int32)


def place_blocks(parts, table):
    columns = parts[0].shape[-1]
    per_part = parts[0].shape[0] // BLOCK
    parts = [part.reshape(per_part, BLOCK, columns) for part in parts]

    def kernel(table_ref, *refs):
        out_ref = refs[-1]
        for at, ref in enumerate(refs[:-1]):
            for b in range(per_part):
                out_ref[table_ref[at * per_part + b]] = ref[b]

    placed = pl.pallas_call(
        kernel,
        out_shape=jax.ShapeDtypeStruct((BLOCKS, BLOCK, columns), parts[0].dtype),
        in_specs=[pl.BlockSpec(memory_space=pltpu.SMEM)]
        + [pl.BlockSpec(memory_space=pltpu.VMEM)] * len(parts),
        out_specs=pl.BlockSpec(memory_space=pltpu.VMEM),
        compiler_params=pltpu.CompilerParams(vmem_limit_bytes=24 * 2**20),
    )(table, *parts)
    return placed.reshape(BLOCKS * BLOCK, columns)


VMEM = pl.BlockSpec(memory_space=pltpu.VMEM)


def softmax_rows(queries, key_rows, positions, score_scale):
    size = queries.shape[0]
    scores = lax.dot_general(
        queries, key_rows, (((1,), (1,)), ((), ())), preferred_element_type=jnp.float32
    )
    i = lax.broadcasted_iota(jnp.int32, (size, size), 0)
    j = lax.broadcasted_iota(jnp.int32, (size, size), 1)
    allowed = (j <= i) & (j >= i - positions)
    weights = jnp.where(allowed, jnp.exp(scores * score_scale), 0.0)
    return weights / jnp.sum(weights, axis=-1, keepdims=True)


def attend(parts, positions, heads, score_scale):
    seq_len, columns = parts[0].shape
    size = columns // (3 * heads)

    def kernel(p0, p1, p2, p3, positions_ref, projected_ref, mixed_ref):
        projected_ref[...] = sum_float32([p0[...], p1[...], p2[...], p3[...]]).astype(jnp.bfloat16)
        for h in range(heads):
            q, k, v = (projected_ref[:, (h * 3 + c) * size : (h * 3 + c + 1) * size] for c in range(3))
            rounded = softmax_rows(q, k, positions_ref[...], score_scale).astype(jnp.bfloat16)
            mixed_ref[:, h * size : (h + 1) * size] = jnp.dot(
                rounded, v, preferred_element_type=jnp.float32
            ).astype(jnp.bfloat16)

    return pl.pallas_call(
        kernel,
        out_shape=(
            jax.ShapeDtypeStruct((seq_len, columns), jnp.bfloat16),
            jax.ShapeDtypeStruct((seq_len, heads * size), jnp.bfloat16),
        ),
        in_specs=[VMEM] * 5,
        out_specs=(VMEM, VMEM),
        compiler_params=pltpu.CompilerParams(vmem_limit_bytes=24 * 2**20),
    )(*parts, positions.reshape(seq_len, 1))


def attend_back(projected, parts, positions, heads, score_scale):
    seq_len, columns = projected.shape
    size = columns // (3 * heads)

    def kernel(projected_ref, p0, p1, p2, p3, positions_ref, out_ref):
        d_mixed = sum_float32([p0[...], p1[...], p2[...], p3[...]]).astype(jnp.bfloat16)
        contract_first = (((0,), (0,)), ((), ()))
        contract_last = (((1,), (1,)), ((), ()))
        for h in range(heads):
            q, k, v = (projected_ref[:, (h * 3 + c) * size : (h * 3 + c + 1) * size] for c in range(3))
            probabilities = softmax_rows(q, k, positions_ref[...], score_scale)
            rounded = probabilities.astype(jnp.bfloat16)
            grad = d_mixed[:, h * size : (h + 1) * size]
            d_probs = lax.dot_general(grad, v, contract_last, preferred_element_type=jnp.float32)
            row_delta = jnp.sum(probabilities * d_probs, axis=-1, keepdims=True)
            d_scores = (probabilities * (d_probs - row_delta) * score_scale).astype(jnp.bfloat16)
            grads = (
                jnp.dot(d_scores, k, preferred_element_type=jnp.float32),
                lax.dot_general(d_scores, q, contract_first, preferred_element_type=jnp.float32),
                lax.dot_general(rounded, grad, contract_first, preferred_element_type=jnp.float32),
            )
            for c in range(3):
                out_ref[:, (h * 3 + c) * size : (h * 3 + c + 1) * size] = grads[c].astype(jnp.bfloat16)

    return pl.pallas_call(
        kernel,
        out_shape=jax.ShapeDtypeStruct((seq_len, columns), jnp.bfloat16),
        in_specs=[VMEM] * 6,
        out_specs=VMEM,
        compiler_params=pltpu.CompilerParams(vmem_limit_bytes=24 * 2**20),
    )(projected, *parts, positions.reshape(seq_len, 1))


def qkv_weight_grad(chunks, grads, heads):
    width, columns = chunks[0].shape[1], grads.shape[1]
    size = columns // (3 * heads)
    step = 512
    rows = chunks[0].shape[0]

    def kernel(c0, c1, c2, c3, grads_ref, out_ref):
        total = None
        for at, ref in enumerate((c0, c1, c2, c3)):
            term = lax.dot_general(
                ref[...],
                grads_ref[at * rows : (at + 1) * rows, :],
                (((0,), (0,)), ((), ())),
                preferred_element_type=jnp.float32,
            )
            total = term if total is None else total + term
        for h in range(heads):
            for c in range(3):
                at = (h * 3 + c) * size
                out_ref[pl.ds(c * heads + h, step, stride=3 * heads), :] = total[:, at : at + size]

    out = pl.pallas_call(
        kernel,
        grid=(width // step,),
        out_shape=jax.ShapeDtypeStruct((width * 3 * heads, size), jnp.float32),
        in_specs=[pl.BlockSpec((rows, step), lambda n: (0, n))] * 4
        + [pl.BlockSpec((4 * rows, columns), lambda n: (0, 0))],
        out_specs=pl.BlockSpec((step * 3 * heads, size), lambda n: (n, 0)),
        compiler_params=pltpu.CompilerParams(vmem_limit_bytes=40 * 2**20),
        cost_estimate=pl.CostEstimate(
            flops=8 * rows * width * columns,
            bytes_accessed=8 * rows * (width + columns) + 4 * width * columns,
            transcendentals=0,
        ),
    )(*chunks, grads)
    return out.reshape(width, 3, heads, size).transpose(0, 2, 1, 3)


def out_weight_grad(mixed, chunks):
    width, columns = chunks[0].shape[1], mixed.shape[1]
    step = 512
    rows = chunks[0].shape[0]

    def kernel(mixed_ref, c0, c1, c2, c3, out_ref):
        total = None
        for at, ref in enumerate((c0, c1, c2, c3)):
            term = lax.dot_general(
                mixed_ref[at * rows : (at + 1) * rows, :],
                ref[...],
                (((0,), (0,)), ((), ())),
                preferred_element_type=jnp.float32,
            )
            total = term if total is None else total + term
        out_ref[...] = total

    return pl.pallas_call(
        kernel,
        grid=(width // step,),
        out_shape=jax.ShapeDtypeStruct((columns, width), jnp.float32),
        in_specs=[pl.BlockSpec((4 * rows, columns), lambda n: (0, 0))]
        + [pl.BlockSpec((rows, step), lambda n: (0, n))] * 4,
        out_specs=pl.BlockSpec((columns, step), lambda n: (0, n)),
        compiler_params=pltpu.CompilerParams(vmem_limit_bytes=40 * 2**20),
        cost_estimate=pl.CostEstimate(
            flops=8 * rows * width * columns,
            bytes_accessed=8 * rows * (width + columns) + 4 * width * columns,
            transcendentals=0,
        ),
    )(mixed, *chunks)


def after(value, *others):
    return lax.optimization_barrier((value,) + others)[0]


def sum_float32(parts):
    total = parts[0].astype(jnp.float32)
    for part in parts[1:]:
        total = total + part.astype(jnp.float32)
    return total


def scatter_plane(term):
    pieces = [None] * 4
    for j in (2, 1, 3, 0):
        other = swap_cores(term(j, 1))
        pair = sum_float32([term(j, 0), other]).astype(jnp.bfloat16)
        pieces[j] = pair if j == 0 else from_ring(pair, 4 - j, False)
        if j == 3:
            last = pair
    column = sum_float32(pieces).astype(jnp.bfloat16).reshape(4, BLOCK, -1)
    parts = [column[0]] + [from_ring(column[i], 4 - i, True) for i in (2, 1, 3)]
    return sum_float32(parts).astype(jnp.bfloat16), last


def scatter_depth(rows, seq_len):
    parts = [rows[:seq_len]]
    for k in (2, 1, 3):
        parts.append(from_depth(rows[k * seq_len : (k + 1) * seq_len], 4 - k))
    return parts


def gather_depth(rows):
    ahead = {k: from_depth(rows, k) for k in (2, 1, 3)}
    return [rows, ahead[1], ahead[2], ahead[3]]


def per_device(tokens, w_qkv, w_out, positions, d_output):
    seq_len = positions.shape[0]
    local_heads = w_qkv.shape[1]
    head_size = w_qkv.shape[3]
    width_part = w_qkv.shape[0]
    score_scale = 1.0 / math.sqrt(head_size)
    out_flat = w_out.reshape(local_heads * head_size, width_part)
    contract_last = (((1,), (1,)), ((), ()))
    depth = lax.axis_index("depth")
    forward, inverse = block_tables(depth)

    both = jnp.concatenate([tokens, d_output], axis=0)
    near = {i: from_ring(both, i, True) for i in OFFSETS}
    near[0] = both
    token_column = jnp.concatenate([near[i][:BLOCK] for i in range(4)], axis=0)
    grad_column = jnp.concatenate([near[i][BLOCK:] for i in range(4)], axis=0)

    own = {j: from_ring(token_column, j, False) for j in OFFSETS}
    own[0] = token_column
    other = {0: swap_cores(token_column)}
    qkv_flat = after(w_qkv, other[0]).reshape(width_part, local_heads * 3 * head_size)
    for j in (1, 3, 2):
        other[j] = swap_cores(own[j])
    token_chunks = [jnp.concatenate([own[j], other[j]], axis=0) for j in range(4)]
    partial = [
        jnp.dot(chunk, qkv_flat, preferred_element_type=jnp.float32).astype(jnp.bfloat16)
        for chunk in token_chunks
    ]
    grad_column = after(grad_column, own[1], own[3])
    own = {j: from_ring(grad_column, j, False) for j in OFFSETS}
    own[0] = grad_column
    rearranged = place_blocks(partial, forward)
    projected_parts = scatter_depth(rearranged, seq_len)

    own[0] = after(own[0], rearranged)
    other = {j: swap_cores(own[j]) for j in range(4)}
    grad_chunks = [jnp.concatenate([own[j], other[j]], axis=0) for j in range(4)]
    d_mixed = place_blocks(
        [
            lax.dot_general(
                chunk, out_flat, contract_last, preferred_element_type=jnp.float32
            ).astype(jnp.bfloat16)
            for chunk in grad_chunks
        ],
        forward,
    )
    d_mixed_parts = scatter_depth(d_mixed, seq_len)

    projected, mixed = attend(projected_parts, positions, local_heads, score_scale)
    heads_all = place_blocks(gather_depth(mixed), inverse)
    d_projected = attend_back(projected, d_mixed_parts, positions, local_heads, score_scale)
    projected_grads = place_blocks(gather_depth(d_projected), inverse)

    half = 4 * BLOCK

    def out_term(j, family):
        at = (j * 2 + family) * half
        return jnp.dot(
            heads_all[at : at + half], out_flat, preferred_element_type=jnp.float32
        ).astype(jnp.bfloat16)

    def token_term(j, family):
        at = (j * 2 + family) * half
        return lax.dot_general(
            projected_grads[at : at + half],
            qkv_flat,
            contract_last,
            preferred_element_type=jnp.float32,
        ).astype(jnp.bfloat16)

    output, _ = scatter_plane(out_term)
    d_tokens, last = scatter_plane(token_term)
    d_out_weight = out_weight_grad(after(heads_all, d_projected), grad_chunks)
    d_out_weight = d_out_weight.reshape(local_heads, head_size, width_part)
    d_qkv_weight = qkv_weight_grad(token_chunks, after(projected_grads, last), local_heads)
    return (output, d_tokens, d_qkv_weight, d_out_weight)


def solution(mesh):
    in_specs = (
        P(("row", "col"), "depth"),
        P("depth", ("row", "col"), None, None),
        P(("row", "col"), None, "depth"),
        P("depth"),
        P(("row", "col"), "depth"),
    )
    out_specs = (
        P(("row", "col"), "depth"),
        P(("row", "col"), "depth"),
        P("depth", ("row", "col"), None, None),
        P(("row", "col"), None, "depth"),
    )
    return jax.shard_map(
        per_device, mesh=mesh, in_specs=in_specs, out_specs=out_specs, check_vma=False
    )
```

```python
import math

import jax
import jax.numpy as jnp
from jax import lax
from jax.experimental import pallas as pl
from jax.experimental.pallas import tpu as pltpu
from jax.sharding import PartitionSpec as P

PLANE = ("row", "col")
BLOCK = 32
BLOCKS = 32
OFFSETS = (1, 3, 2)
SENDS = (2, 1, 3, 0)
VMEM = pl.BlockSpec(memory_space=pltpu.VMEM)
NO_COST = pl.CostEstimate(flops=0, bytes_accessed=0, transcendentals=0)


def plane_index(x, y, core):
    return ((x % 2) * 2 + core) * 8 + (x // 2) * 4 + y


def ring_pairs(offset, first):
    pairs = []
    for x in range(4):
        for y in range(4):
            for core in range(2):
                along_x = (core == 0) == first
                sx, sy = ((x + offset) % 4, y) if along_x else (x, (y + offset) % 4)
                pairs.append((plane_index(sx, sy, core), plane_index(x, y, core)))
    return pairs


def core_pairs():
    return [
        (plane_index(x, y, core), plane_index(x, y, 1 - core))
        for x in range(4)
        for y in range(4)
        for core in range(2)
    ]


def depth_pairs(offset):
    return [((z + offset) % 4, z) for z in range(4)]


def swap_cores(rows):
    return lax.ppermute(rows, PLANE, core_pairs())


def from_ring(rows, offset, first):
    return lax.ppermute(rows, PLANE, ring_pairs(offset, first))


def from_depth(rows, offset):
    return lax.ppermute(rows, "depth", depth_pairs(offset))


def block_tables(depth):
    row, col = lax.axis_index("row"), lax.axis_index("col")
    x, y, core = (col // 4) * 2 + row // 2, col % 4, row % 2
    place = jnp.arange(BLOCKS, dtype=jnp.int32)
    j, family, i = place // 8, (place // 4) % 2, place % 4
    j = jnp.where(j >= 2, 5 - j, j)
    of_core = (core + family) % 2
    dx, dy = jnp.where(of_core == 0, i, j), jnp.where(of_core == 0, j, i)
    sx, sy = (x + dx) % 4, (y + dy) % 4
    sequence = (sx % 2) * 2 + of_core
    forward = ((sequence - depth + 4) % 4) * 8 + (sx // 2) * 4 + sy
    sequence = (place // 8 + depth) % 4
    of_core = sequence % 2
    sx, sy = ((place % 8) // 4) * 2 + sequence // 2, place % 4
    family = (of_core + core) % 2
    dx, dy = (sx - x + 4) % 4, (sy - y + 4) % 4
    i, j = jnp.where(of_core == 0, dx, dy), jnp.where(of_core == 0, dy, dx)
    inverse = family * 16 + jnp.where(j == 0, 3, jnp.where(j == 2, 0, (j + 1) // 2)) * 4 + i
    return forward.astype(jnp.int32), inverse.astype(jnp.int32)


def place_blocks(parts, table, outs=1):
    columns = parts[0].shape[-1]
    per_part, per_out = BLOCKS // len(parts), BLOCKS // outs
    parts = [part.reshape(-1, BLOCK, columns) for part in parts]

    def kernel(table_ref, *refs):
        *refs, placed = refs
        for at, ref in enumerate(refs[: len(parts)]):
            for b in range(per_part):
                placed[table_ref[at * per_part + b]] = ref[b]
        for k, ref in enumerate(refs[len(parts) :]):
            ref[...] = placed[k * per_out : (k + 1) * per_out]

    placed = pl.pallas_call(
        kernel,
        out_shape=(jax.ShapeDtypeStruct((per_out, BLOCK, columns), parts[0].dtype),) * outs,
        in_specs=[pl.BlockSpec(memory_space=pltpu.SMEM)] + [VMEM] * len(parts),
        out_specs=(VMEM,) * outs,
        scratch_shapes=[pltpu.VMEM((BLOCKS, BLOCK, columns), parts[0].dtype)],
        compiler_params=pltpu.CompilerParams(vmem_limit_bytes=24 * 2**20),
        cost_estimate=NO_COST,
    )(table, *parts)
    return [out.reshape(per_out * BLOCK, columns) for out in placed]


def softmax_rows(queries, key_rows, positions, score_scale):
    size = queries.shape[0]
    scores = lax.dot_general(
        queries, key_rows, (((1,), (1,)), ((), ())), preferred_element_type=jnp.float32
    )
    i = lax.broadcasted_iota(jnp.int32, (size, size), 0)
    j = lax.broadcasted_iota(jnp.int32, (size, size), 1)
    allowed = (j <= i) & (j >= i - positions)
    weights = jnp.where(allowed, jnp.exp(scores * score_scale), 0.0)
    return weights / jnp.sum(weights, axis=-1, keepdims=True)


def attend(parts, d_mixed, positions, heads, score_scale):
    seq_len, columns = parts[0].shape
    size = columns // (3 * heads)
    width = heads * size

    def kernel(p0, p1, p2, p3, d1, d2, d3, positions_ref, projected_ref, mixed_ref, *sends):
        projected_ref[...] = sum_float32([p0[...], p1[...], p2[...], p3[...]]).astype(jnp.bfloat16)
        for h in range(heads):
            q, k, v = (projected_ref[:, (h * 3 + c) * size : (h * 3 + c + 1) * size] for c in range(3))
            rounded = softmax_rows(q, k, positions_ref[...], score_scale).astype(jnp.bfloat16)
            mixed_ref[:, h * size : (h + 1) * size] = jnp.dot(
                rounded, v, preferred_element_type=jnp.float32
            ).astype(jnp.bfloat16)
        for d_mixed_ref, ref in zip((d1, d2, d3), sends):
            ref[:seq_len] = mixed_ref[...]
            ref[seq_len:] = d_mixed_ref[...]

    return pl.pallas_call(
        kernel,
        out_shape=(
            jax.ShapeDtypeStruct((seq_len, columns), jnp.bfloat16),
            jax.ShapeDtypeStruct((seq_len, width), jnp.bfloat16),
        )
        + (jax.ShapeDtypeStruct((2 * seq_len, width), jnp.bfloat16),) * 3,
        in_specs=[VMEM] * 8,
        out_specs=(VMEM,) * 5,
        compiler_params=pltpu.CompilerParams(vmem_limit_bytes=24 * 2**20),
        cost_estimate=NO_COST,
    )(*parts, *d_mixed[1:], positions.reshape(seq_len, 1))


def attend_back(projected, parts, positions, heads, score_scale):
    seq_len, columns = projected.shape
    size = columns // (3 * heads)

    def kernel(projected_ref, p0, p1, p2, p3, positions_ref, out_ref):
        d_mixed = sum_float32([p0[:seq_len]] + [p[seq_len:] for p in (p1, p2, p3)]).astype(jnp.bfloat16)
        contract_first = (((0,), (0,)), ((), ()))
        contract_last = (((1,), (1,)), ((), ()))
        for h in range(heads):
            q, k, v = (projected_ref[:, (h * 3 + c) * size : (h * 3 + c + 1) * size] for c in range(3))
            probabilities = softmax_rows(q, k, positions_ref[...], score_scale)
            rounded = probabilities.astype(jnp.bfloat16)
            grad = d_mixed[:, h * size : (h + 1) * size]
            d_probs = lax.dot_general(grad, v, contract_last, preferred_element_type=jnp.float32)
            row_delta = jnp.sum(probabilities * d_probs, axis=-1, keepdims=True)
            d_scores = (probabilities * (d_probs - row_delta) * score_scale).astype(jnp.bfloat16)
            grads = (
                jnp.dot(d_scores, k, preferred_element_type=jnp.float32),
                lax.dot_general(d_scores, q, contract_first, preferred_element_type=jnp.float32),
                lax.dot_general(rounded, grad, contract_first, preferred_element_type=jnp.float32),
            )
            for c in range(3):
                out_ref[:, (h * 3 + c) * size : (h * 3 + c + 1) * size] = grads[c].astype(jnp.bfloat16)

    return pl.pallas_call(
        kernel,
        out_shape=jax.ShapeDtypeStruct((seq_len, columns), jnp.bfloat16),
        in_specs=[VMEM] * 6,
        out_specs=VMEM,
        compiler_params=pltpu.CompilerParams(vmem_limit_bytes=24 * 2**20),
        cost_estimate=NO_COST,
    )(projected, *parts, positions.reshape(seq_len, 1))


def chunk_rows(ref, j):
    half = 4 * BLOCK
    at = SENDS.index(j) * half
    return jnp.concatenate([ref[at : at + half, :], ref[at + 4 * half : at + 5 * half, :]], axis=0)


def transposed_product(left, right):
    return lax.dot_general(
        left, right, (((0,), (0,)), ((), ())), preferred_element_type=jnp.float32
    )


def grad_cost(chunks, columns):
    rows, width = chunks[0].shape
    return pl.CostEstimate(
        flops=8 * rows * width * columns,
        bytes_accessed=8 * rows * (width + columns) + 4 * width * columns,
        transcendentals=0,
    )


def qkv_weight_grad(chunks, grads, heads):
    rows, width = chunks[0].shape
    columns = grads.shape[1]
    size = columns // (3 * heads)
    step = 512

    def kernel(c0, c1, c2, c3, grads_ref, out_ref):
        total = transposed_product(c0[...], chunk_rows(grads_ref, 0))
        for j, ref in enumerate((c1, c2, c3), 1):
            total = total + transposed_product(ref[...], chunk_rows(grads_ref, j))
        for h in range(heads):
            for c in range(3):
                at = (h * 3 + c) * size
                out_ref[pl.ds(c * heads + h, step, stride=3 * heads), :] = total[:, at : at + size]

    out = pl.pallas_call(
        kernel,
        grid=(width // step,),
        out_shape=jax.ShapeDtypeStruct((width * 3 * heads, size), jnp.float32),
        in_specs=[pl.BlockSpec((rows, step), lambda n: (0, n))] * 4
        + [pl.BlockSpec((4 * rows, columns), lambda n: (0, 0))],
        out_specs=pl.BlockSpec((step * 3 * heads, size), lambda n: (n, 0)),
        compiler_params=pltpu.CompilerParams(vmem_limit_bytes=40 * 2**20),
        cost_estimate=grad_cost(chunks, columns),
    )(*chunks, grads)
    return out.reshape(width, 3, heads, size).transpose(0, 2, 1, 3)


def out_weight_grad(mixed, chunks):
    rows, width = chunks[0].shape
    columns = mixed.shape[1]
    step = 512

    def kernel(mixed_ref, c0, c1, c2, c3, out_ref):
        total = transposed_product(chunk_rows(mixed_ref, 0), c0[...])
        for j, ref in enumerate((c1, c2, c3), 1):
            total = total + transposed_product(chunk_rows(mixed_ref, j), ref[...])
        out_ref[...] = total

    return pl.pallas_call(
        kernel,
        grid=(width // step,),
        out_shape=jax.ShapeDtypeStruct((columns, width), jnp.float32),
        in_specs=[pl.BlockSpec((4 * rows, columns), lambda n: (0, 0))]
        + [pl.BlockSpec((rows, step), lambda n: (0, n))] * 4,
        out_specs=pl.BlockSpec((columns, step), lambda n: (0, n)),
        compiler_params=pltpu.CompilerParams(vmem_limit_bytes=40 * 2**20),
        cost_estimate=grad_cost(chunks, columns),
    )(mixed, *chunks)


def after(value, *others):
    return lax.optimization_barrier((value,) + others)[0]


def sum_float32(parts):
    total = parts[0].astype(jnp.float32)
    for part in parts[1:]:
        total = total + part.astype(jnp.float32)
    return total


def pair_sums(own_term, others):
    return {j: sum_float32([own_term(j), others[j]]).astype(jnp.bfloat16) for j in SENDS}


def through_neighbours(own):
    half = own[1].shape[0] // 2
    return jnp.concatenate(
        [from_ring(own[1][:half], 1, False), from_ring(own[3][half:], 3, False)], axis=0
    )


def scatter_near(*columns):
    sums = [sum_float32(pieces).astype(jnp.bfloat16) for pieces in columns]

    def part(i):
        return jnp.concatenate([rows[i * BLOCK : (i + 1) * BLOCK] for rows in sums], axis=0)

    parts = [part(0)] + [from_ring(part(i), 4 - i, True) for i in (2, 1, 3)]
    total = sum_float32(parts).astype(jnp.bfloat16)
    return [total[at * BLOCK : (at + 1) * BLOCK] for at in range(len(columns))]


def scatter_depth(blocks):
    return [blocks[0]] + [from_depth(blocks[k], 4 - k) for k in (1, 2, 3)]


def gather_depth(rows):
    ahead = {k: from_depth(rows, k) for k in (2, 1, 3)}
    return [rows, ahead[1], ahead[2], ahead[3]]


def per_device(tokens, w_qkv, w_out, positions, d_output):
    seq_len = positions.shape[0]
    local_heads = w_qkv.shape[1]
    head_size = w_qkv.shape[3]
    width_part = w_qkv.shape[0]
    score_scale = 1.0 / math.sqrt(head_size)
    out_flat = w_out.reshape(local_heads * head_size, width_part)
    contract_last = (((1,), (1,)), ((), ()))
    depth = lax.axis_index("depth")
    forward, inverse = block_tables(depth)

    near = {i: from_ring(tokens, i, True) for i in OFFSETS}
    near_grads = {i: from_ring(d_output, i, True) for i in (1, 3)}
    near[0] = tokens
    token_column = jnp.concatenate([near[i] for i in range(4)], axis=0)
    token_column = after(token_column, near_grads[1], near_grads[3])
    own = {0: token_column}
    own[1] = from_ring(token_column, 1, False)
    own[3] = from_ring(token_column, 3, False)
    other = {0: swap_cores(token_column)}
    qkv_flat = after(w_qkv, token_column).reshape(width_part, local_heads * 3 * head_size).T
    own[1], own[3], grad_rows = after((own[1], own[3], d_output), qkv_flat, other[0])
    own[2] = through_neighbours(own)
    near_grads[2] = from_ring(grad_rows, 2, True)
    near_grads[0] = d_output
    other[1] = swap_cores(own[1])

    def product(chunk, weight):
        return lax.dot_general(
            chunk, weight, contract_last, preferred_element_type=jnp.float32
        ).astype(jnp.bfloat16)

    chunks = {j: jnp.concatenate([own[j], other[j]], axis=0) for j in (0, 1)}
    parts = [product(chunks[0], qkv_flat)]
    own[2], own[3] = after((own[2], own[3]), near_grads[2], parts[0], other[1])
    for j in (3, 2):
        other[j] = swap_cores(own[j])
        chunks[j] = jnp.concatenate([own[j], other[j]], axis=0)
    parts += [product(chunks[j], qkv_flat) for j in (1, 3, 2)]
    parts = place_blocks(parts, forward, 4)

    grad_column = jnp.concatenate([near_grads[i] for i in range(4)], axis=0)
    grad_column = after(grad_column, own[2])
    own_grads = {j: from_ring(grad_column, j, False) for j in (1, 3)}
    own_grads[0] = grad_column
    other_grads = {0: swap_cores(grad_column)}
    parts[1], parts[3] = after((parts[1], parts[3]), other_grads[0])
    parts[2] = after(parts[2], own_grads[1], own_grads[3])
    projected_parts = scatter_depth(parts)
    own_grads[2] = through_neighbours(own_grads)
    own_grads[1], own_grads[3] = after((own_grads[1], own_grads[3]), own_grads[2])
    for j in (1, 3, 2):
        other_grads[j] = swap_cores(own_grads[j])
    grad_chunks = {
        j: jnp.concatenate([own_grads[j], other_grads[j]], axis=0) for j in range(4)
    }
    d_mixed = place_blocks(
        [product(grad_chunks[j], out_flat) for j in (0, 1, 3, 2)], forward, 4
    )

    projected, mixed, *sends = attend(
        projected_parts, d_mixed, positions, local_heads, score_scale
    )
    behind = [from_depth(sends[k - 1], 4 - k) for k in (1, 2, 3)]
    (heads_all,) = place_blocks([mixed] + behind[::-1], inverse)
    half = 4 * BLOCK
    out_others = jnp.dot(
        heads_all[4 * half :], out_flat, preferred_element_type=jnp.float32
    ).astype(jnp.bfloat16)
    d_projected = attend_back(
        after(projected, out_others), [d_mixed[0]] + behind, positions, local_heads, score_scale
    )

    out_others = swap_cores(after(out_others, d_projected))

    def out_term(j):
        at = SENDS.index(j) * half
        return jnp.dot(
            heads_all[at : at + half], out_flat, preferred_element_type=jnp.float32
        ).astype(jnp.bfloat16)

    out_pairs = pair_sums(
        out_term,
        {j: out_others[SENDS.index(j) * half : (SENDS.index(j) + 1) * half] for j in SENDS},
    )
    passed = [
        from_ring(out_pairs[2][: half // 2], 3, False),
        from_ring(out_pairs[2][half // 2 :], 1, False),
    ]
    grad_parts = gather_depth(d_projected)
    ahead = jnp.concatenate(
        [sum_float32([out_pairs[1][: half // 2], passed[0]]).astype(jnp.bfloat16), out_pairs[1][half // 2 :]]
    )
    behind = jnp.concatenate(
        [out_pairs[3][: half // 2], sum_float32([out_pairs[3][half // 2 :], passed[1]]).astype(jnp.bfloat16)]
    )
    grad_parts[2], ahead, behind = after((grad_parts[2], ahead, behind))
    (projected_grads,) = place_blocks(grad_parts, inverse)
    out_pieces = [out_pairs[0], from_ring(ahead, 3, False), from_ring(behind, 1, False)]

    def token_term(start, rows):
        return jnp.dot(
            projected_grads[start : start + rows], qkv_flat, preferred_element_type=jnp.float32
        ).astype(jnp.bfloat16)

    first = swap_cores(token_term(4 * half, half))
    second = swap_cores(token_term(5 * half, 3 * half))
    token_pairs = pair_sums(
        lambda j: token_term(SENDS.index(j) * half, half),
        {2: first, 1: second[:half], 3: second[half : 2 * half], 0: second[2 * half :]},
    )
    token_pairs[2], token_pairs[1], token_pairs[3] = after(
        (token_pairs[2], token_pairs[1], token_pairs[3]), *out_pieces
    )
    token_pieces = [from_ring(token_pairs[j], 4 - j, False) for j in (2, 1, 3)]
    d_out_weight = out_weight_grad(
        after(heads_all, token_pairs[3]), [grad_chunks[j] for j in range(4)]
    )
    d_qkv_weight = qkv_weight_grad(
        [chunks[j] for j in range(4)], after(projected_grads, token_pairs[3]), local_heads
    )
    token_pieces.append(after(token_pairs[0], d_out_weight, d_qkv_weight))
    output, d_tokens = scatter_near(out_pieces, token_pieces)
    d_out_weight = d_out_weight.reshape(local_heads, head_size, width_part)
    return (output, d_tokens, d_qkv_weight, d_out_weight)


def solution(mesh):
    in_specs = (
        P(("row", "col"), "depth"),
        P("depth", ("row", "col"), None, None),
        P(("row", "col"), None, "depth"),
        P("depth"),
        P(("row", "col"), "depth"),
    )
    out_specs = (
        P(("row", "col"), "depth"),
        P(("row", "col"), "depth"),
        P("depth", ("row", "col"), None, None),
        P(("row", "col"), None, "depth"),
    )
    return jax.shard_map(
        per_device, mesh=mesh, in_specs=in_specs, out_specs=out_specs, check_vma=False
    )
```

```python
import math

import jax
import jax.numpy as jnp
from jax import lax
from jax.experimental import pallas as pl
from jax.experimental.pallas import tpu as pltpu
from jax.sharding import PartitionSpec as P

PLANE = ("row", "col")
BLOCK = 32
BLOCKS = 32
OFFSETS = (1, 3, 2)
SENDS = (2, 1, 3, 0)
VMEM = pl.BlockSpec(memory_space=pltpu.VMEM)
NO_COST = pl.CostEstimate(flops=0, bytes_accessed=0, transcendentals=0)


def plane_index(x, y, core):
    return ((x % 2) * 2 + core) * 8 + (x // 2) * 4 + y


def ring_pairs(offset, first):
    pairs = []
    for x in range(4):
        for y in range(4):
            for core in range(2):
                along_x = (core == 0) == first
                sx, sy = ((x + offset) % 4, y) if along_x else (x, (y + offset) % 4)
                pairs.append((plane_index(sx, sy, core), plane_index(x, y, core)))
    return pairs


def core_pairs():
    return [
        (plane_index(x, y, core), plane_index(x, y, 1 - core))
        for x in range(4)
        for y in range(4)
        for core in range(2)
    ]


def depth_pairs(offset):
    return [((z + offset) % 4, z) for z in range(4)]


def swap_cores(rows):
    return lax.ppermute(rows, PLANE, core_pairs())


def from_ring(rows, offset, first):
    return lax.ppermute(rows, PLANE, ring_pairs(offset, first))


def from_depth(rows, offset):
    return lax.ppermute(rows, "depth", depth_pairs(offset))


def block_tables(depth):
    row, col = lax.axis_index("row"), lax.axis_index("col")
    x, y, core = (col // 4) * 2 + row // 2, col % 4, row % 2
    place = jnp.arange(BLOCKS, dtype=jnp.int32)
    j, family, i = place // 8, (place // 4) % 2, place % 4
    j = jnp.where(j >= 2, 5 - j, j)
    of_core = (core + family) % 2
    dx, dy = jnp.where(of_core == 0, i, j), jnp.where(of_core == 0, j, i)
    sx, sy = (x + dx) % 4, (y + dy) % 4
    sequence = (sx % 2) * 2 + of_core
    forward = ((sequence - depth + 4) % 4) * 8 + (sx // 2) * 4 + sy
    sequence = (place // 8 + depth) % 4
    of_core = sequence % 2
    sx, sy = ((place % 8) // 4) * 2 + sequence // 2, place % 4
    family = (of_core + core) % 2
    dx, dy = (sx - x + 4) % 4, (sy - y + 4) % 4
    i, j = jnp.where(of_core == 0, dx, dy), jnp.where(of_core == 0, dy, dx)
    inverse = family * 16 + jnp.where(j == 0, 3, jnp.where(j == 2, 0, (j + 1) // 2)) * 4 + i
    return forward.astype(jnp.int32), inverse.astype(jnp.int32)


def place_blocks(parts, table, outs=1):
    columns = parts[0].shape[-1]
    per_part, per_out = BLOCKS // len(parts), BLOCKS // outs
    parts = [part.reshape(-1, BLOCK, columns) for part in parts]

    def kernel(table_ref, *refs):
        *refs, placed = refs
        for at, ref in enumerate(refs[: len(parts)]):
            for b in range(per_part):
                placed[table_ref[at * per_part + b]] = ref[b]
        for k, ref in enumerate(refs[len(parts) :]):
            ref[...] = placed[k * per_out : (k + 1) * per_out]

    placed = pl.pallas_call(
        kernel,
        out_shape=(jax.ShapeDtypeStruct((per_out, BLOCK, columns), parts[0].dtype),) * outs,
        in_specs=[pl.BlockSpec(memory_space=pltpu.SMEM)] + [VMEM] * len(parts),
        out_specs=(VMEM,) * outs,
        scratch_shapes=[pltpu.VMEM((BLOCKS, BLOCK, columns), parts[0].dtype)],
        compiler_params=pltpu.CompilerParams(vmem_limit_bytes=24 * 2**20),
        cost_estimate=NO_COST,
    )(table, *parts)
    return [out.reshape(per_out * BLOCK, columns) for out in placed]


def softmax_rows(queries, key_rows, positions, score_scale):
    size = queries.shape[0]
    scores = lax.dot_general(
        queries, key_rows, (((1,), (1,)), ((), ())), preferred_element_type=jnp.float32
    )
    i = lax.broadcasted_iota(jnp.int32, (size, size), 0)
    j = lax.broadcasted_iota(jnp.int32, (size, size), 1)
    allowed = (j <= i) & (j >= i - positions)
    weights = jnp.where(allowed, jnp.exp(scores * score_scale), 0.0)
    return weights / jnp.sum(weights, axis=-1, keepdims=True)


def attend(parts, d_mixed, positions, heads, score_scale):
    seq_len, columns = parts[0].shape
    size = columns // (3 * heads)
    width = heads * size

    def kernel(p0, p1, p2, p3, d1, d2, d3, positions_ref, projected_ref, mixed_ref, *sends):
        projected_ref[...] = sum_float32([p0[...], p1[...], p2[...], p3[...]]).astype(jnp.bfloat16)
        for h in range(heads):
            q, k, v = (projected_ref[:, (h * 3 + c) * size : (h * 3 + c + 1) * size] for c in range(3))
            rounded = softmax_rows(q, k, positions_ref[...], score_scale).astype(jnp.bfloat16)
            mixed_ref[:, h * size : (h + 1) * size] = jnp.dot(
                rounded, v, preferred_element_type=jnp.float32
            ).astype(jnp.bfloat16)
        for d_mixed_ref, ref in zip((d1, d2, d3), sends):
            ref[:seq_len] = mixed_ref[...]
            ref[seq_len:] = d_mixed_ref[...]

    return pl.pallas_call(
        kernel,
        out_shape=(
            jax.ShapeDtypeStruct((seq_len, columns), jnp.bfloat16),
            jax.ShapeDtypeStruct((seq_len, width), jnp.bfloat16),
        )
        + (jax.ShapeDtypeStruct((2 * seq_len, width), jnp.bfloat16),) * 3,
        in_specs=[VMEM] * 8,
        out_specs=(VMEM,) * 5,
        compiler_params=pltpu.CompilerParams(vmem_limit_bytes=24 * 2**20),
        cost_estimate=NO_COST,
    )(*parts, *d_mixed[1:], positions.reshape(seq_len, 1))


def attend_back(projected, parts, positions, heads, score_scale):
    seq_len, columns = projected.shape
    size = columns // (3 * heads)

    def kernel(projected_ref, p0, p1, p2, p3, positions_ref, out_ref):
        d_mixed = sum_float32([p0[:seq_len]] + [p[seq_len:] for p in (p1, p2, p3)]).astype(jnp.bfloat16)
        contract_first = (((0,), (0,)), ((), ()))
        contract_last = (((1,), (1,)), ((), ()))
        for h in range(heads):
            q, k, v = (projected_ref[:, (h * 3 + c) * size : (h * 3 + c + 1) * size] for c in range(3))
            probabilities = softmax_rows(q, k, positions_ref[...], score_scale)
            rounded = probabilities.astype(jnp.bfloat16)
            grad = d_mixed[:, h * size : (h + 1) * size]
            d_probs = lax.dot_general(grad, v, contract_last, preferred_element_type=jnp.float32)
            row_delta = jnp.sum(probabilities * d_probs, axis=-1, keepdims=True)
            d_scores = (probabilities * (d_probs - row_delta) * score_scale).astype(jnp.bfloat16)
            grads = (
                jnp.dot(d_scores, k, preferred_element_type=jnp.float32),
                lax.dot_general(d_scores, q, contract_first, preferred_element_type=jnp.float32),
                lax.dot_general(rounded, grad, contract_first, preferred_element_type=jnp.float32),
            )
            for c in range(3):
                out_ref[:, (h * 3 + c) * size : (h * 3 + c + 1) * size] = grads[c].astype(jnp.bfloat16)

    return pl.pallas_call(
        kernel,
        out_shape=jax.ShapeDtypeStruct((seq_len, columns), jnp.bfloat16),
        in_specs=[VMEM] * 6,
        out_specs=VMEM,
        compiler_params=pltpu.CompilerParams(vmem_limit_bytes=24 * 2**20),
        cost_estimate=NO_COST,
    )(projected, *parts, positions.reshape(seq_len, 1))


def chunk_rows(ref, j):
    half = 4 * BLOCK
    at = SENDS.index(j) * half
    return jnp.concatenate([ref[at : at + half, :], ref[at + 4 * half : at + 5 * half, :]], axis=0)


def transposed_product(left, right):
    return lax.dot_general(
        left, right, (((0,), (0,)), ((), ())), preferred_element_type=jnp.float32
    )


def grad_cost(chunks, columns):
    rows, width = chunks[0].shape
    return pl.CostEstimate(
        flops=8 * rows * width * columns,
        bytes_accessed=8 * rows * (width + columns) + 4 * width * columns,
        transcendentals=0,
    )


def qkv_weight_grad(chunks, grads, heads):
    rows, width = chunks[0].shape
    columns = grads.shape[1]
    size = columns // (3 * heads)
    step = 512

    def kernel(c0, c1, c2, c3, grads_ref, out_ref):
        total = transposed_product(c0[...], chunk_rows(grads_ref, 0))
        for j, ref in enumerate((c1, c2, c3), 1):
            total = total + transposed_product(ref[...], chunk_rows(grads_ref, j))
        for h in range(heads):
            for c in range(3):
                at = (h * 3 + c) * size
                out_ref[pl.ds(c * heads + h, step, stride=3 * heads), :] = total[:, at : at + size]

    out = pl.pallas_call(
        kernel,
        grid=(width // step,),
        out_shape=jax.ShapeDtypeStruct((width * 3 * heads, size), jnp.float32),
        in_specs=[pl.BlockSpec((rows, step), lambda n: (0, n))] * 4
        + [pl.BlockSpec((4 * rows, columns), lambda n: (0, 0))],
        out_specs=pl.BlockSpec((step * 3 * heads, size), lambda n: (n, 0)),
        compiler_params=pltpu.CompilerParams(vmem_limit_bytes=24 * 2**20),
        cost_estimate=grad_cost(chunks, columns),
    )(*chunks, grads)
    return out.reshape(width, 3, heads, size).transpose(0, 2, 1, 3)


def out_weight_grad(mixed, chunks):
    rows, width = chunks[0].shape
    columns = mixed.shape[1]
    step = 512

    def kernel(mixed_ref, c0, c1, c2, c3, out_ref):
        total = transposed_product(chunk_rows(mixed_ref, 0), c0[...])
        for j, ref in enumerate((c1, c2, c3), 1):
            total = total + transposed_product(chunk_rows(mixed_ref, j), ref[...])
        out_ref[...] = total

    return pl.pallas_call(
        kernel,
        grid=(width // step,),
        out_shape=jax.ShapeDtypeStruct((columns, width), jnp.float32),
        in_specs=[pl.BlockSpec((4 * rows, columns), lambda n: (0, 0))]
        + [pl.BlockSpec((rows, step), lambda n: (0, n))] * 4,
        out_specs=pl.BlockSpec((columns, step), lambda n: (0, n)),
        compiler_params=pltpu.CompilerParams(vmem_limit_bytes=12 * 2**20),
        cost_estimate=grad_cost(chunks, columns),
    )(mixed, *chunks)


def after(value, *others):
    return lax.optimization_barrier((value,) + others)[0]


def sum_float32(parts):
    total = parts[0].astype(jnp.float32)
    for part in parts[1:]:
        total = total + part.astype(jnp.float32)
    return total


def pair_sums(own_term, others):
    return {j: sum_float32([own_term(j), others[j]]).astype(jnp.bfloat16) for j in SENDS}


def through_neighbours(own):
    half = own[1].shape[0] // 2
    return jnp.concatenate(
        [from_ring(own[1][:half], 1, False), from_ring(own[3][half:], 3, False)], axis=0
    )


def pass_on(pairs):
    half = pairs[2].shape[0] // 2
    return [from_ring(pairs[2][:half], 3, False), from_ring(pairs[2][half:], 1, False)]


def add_passed(pairs, passed):
    half = pairs[2].shape[0] // 2
    first = sum_float32([pairs[1][:half], passed[0]]).astype(jnp.bfloat16)
    last = sum_float32([pairs[3][half:], passed[1]]).astype(jnp.bfloat16)
    ahead = jnp.concatenate([first, pairs[1][half:]], axis=0)
    behind = jnp.concatenate([pairs[3][:half], last], axis=0)
    return ahead, behind


def scatter_near(*columns):
    sums = [sum_float32(pieces).astype(jnp.bfloat16) for pieces in columns]

    def part(i):
        return jnp.concatenate([rows[i * BLOCK : (i + 1) * BLOCK] for rows in sums], axis=0)

    parts = [part(0)] + [from_ring(part(i), 4 - i, True) for i in (2, 1, 3)]
    total = sum_float32(parts).astype(jnp.bfloat16)
    return [total[at * BLOCK : (at + 1) * BLOCK] for at in range(len(columns))]


def scatter_depth(blocks):
    return [blocks[0]] + [from_depth(blocks[k], 4 - k) for k in (1, 2, 3)]


def gather_depth(rows):
    ahead = {k: from_depth(rows, k) for k in (2, 1, 3)}
    return [rows, ahead[1], ahead[2], ahead[3]]


def per_device(tokens, w_qkv, w_out, positions, d_output):
    seq_len = positions.shape[0]
    local_heads = w_qkv.shape[1]
    head_size = w_qkv.shape[3]
    width_part = w_qkv.shape[0]
    score_scale = 1.0 / math.sqrt(head_size)
    out_flat = w_out.reshape(local_heads * head_size, width_part)
    contract_last = (((1,), (1,)), ((), ()))
    depth = lax.axis_index("depth")
    forward, inverse = block_tables(depth)

    near = {i: from_ring(tokens, i, True) for i in OFFSETS}
    near_grads = {i: from_ring(d_output, i, True) for i in (1, 3)}
    near[0] = tokens
    token_column = jnp.concatenate([near[i] for i in range(4)], axis=0)
    token_column = after(token_column, near_grads[1], near_grads[3])
    own = {j: from_ring(token_column, j, False) for j in OFFSETS}
    own[0] = token_column
    other = {0: swap_cores(token_column)}
    qkv_flat = after(w_qkv, token_column).reshape(width_part, local_heads * 3 * head_size).T
    near_grads[2] = from_ring(after(d_output, token_column), 2, True)
    near_grads[0] = d_output
    own[1], own[3] = after((own[1], own[3]), qkv_flat, other[0], near_grads[2])

    def product(chunk, weight):
        return lax.dot_general(
            chunk, weight, contract_last, preferred_element_type=jnp.float32
        ).astype(jnp.bfloat16)

    chunks = {0: jnp.concatenate([own[0], other[0]], axis=0)}
    parts = [product(chunks[0], qkv_flat)]
    grad_column = jnp.concatenate([near_grads[i] for i in range(4)], axis=0)
    other[1], other[3] = swap_cores(own[1]), swap_cores(own[3])
    own[2], grad_column = after((own[2], grad_column), parts[0], other[1], other[3])
    other[2] = swap_cores(own[2])
    for j in OFFSETS:
        chunks[j] = jnp.concatenate([own[j], other[j]], axis=0)
    parts += [product(chunks[j], qkv_flat) for j in (1, 3, 2)]
    parts = place_blocks(parts, forward, 4)

    grad_column = after(grad_column, own[2])
    own_grads = {j: from_ring(grad_column, j, False) for j in (1, 3)}
    own_grads[0] = grad_column
    other_grads = {0: swap_cores(grad_column)}
    parts[1], parts[3] = after((parts[1], parts[3]), other_grads[0])
    parts[2] = after(parts[2], own_grads[1], own_grads[3])
    projected_parts = scatter_depth(parts)
    own_grads[1], own_grads[3] = after((own_grads[1], own_grads[3]), parts[0])
    own_grads[2] = through_neighbours(own_grads)
    own_grads[1], own_grads[3] = after((own_grads[1], own_grads[3]), own_grads[2])
    for j in (1, 3, 2):
        other_grads[j] = swap_cores(own_grads[j])
    grad_chunks = {
        j: jnp.concatenate([own_grads[j], other_grads[j]], axis=0) for j in range(4)
    }
    d_mixed = place_blocks(
        [product(grad_chunks[j], out_flat) for j in (0, 1, 3, 2)], forward, 4
    )

    projected, mixed, *sends = attend(
        projected_parts, d_mixed, positions, local_heads, score_scale
    )
    behind = [from_depth(sends[k - 1], 4 - k) for k in (1, 2, 3)]
    (heads_all,) = place_blocks([mixed] + behind[::-1], inverse)
    half = 4 * BLOCK
    out_others = jnp.dot(
        heads_all[4 * half :], out_flat, preferred_element_type=jnp.float32
    ).astype(jnp.bfloat16)
    d_projected = attend_back(
        after(projected, out_others), [d_mixed[0]] + behind, positions, local_heads, score_scale
    )

    out_others = swap_cores(after(out_others, d_projected))

    def out_term(j):
        at = SENDS.index(j) * half
        return jnp.dot(
            heads_all[at : at + half], out_flat, preferred_element_type=jnp.float32
        ).astype(jnp.bfloat16)

    out_pairs = pair_sums(
        out_term,
        {j: out_others[SENDS.index(j) * half : (SENDS.index(j) + 1) * half] for j in SENDS},
    )
    passed = pass_on(out_pairs)
    grad_parts = gather_depth(d_projected)
    ahead, behind = add_passed(out_pairs, passed)
    grad_parts[2], ahead, behind = after((grad_parts[2], ahead, behind))
    (projected_grads,) = place_blocks(grad_parts, inverse)
    out_pieces = [out_pairs[0], from_ring(ahead, 3, False), from_ring(behind, 1, False)]

    def token_term(start, rows):
        return jnp.dot(
            projected_grads[start : start + rows], qkv_flat, preferred_element_type=jnp.float32
        ).astype(jnp.bfloat16)

    first = token_term(4 * half, half)
    projected_grads = after(projected_grads, first)
    first = swap_cores(first)
    second = swap_cores(token_term(5 * half, 3 * half))
    token_pairs = pair_sums(
        lambda j: token_term(SENDS.index(j) * half, half),
        {2: first, 1: second[:half], 3: second[half : 2 * half], 0: second[2 * half :]},
    )
    passed = pass_on(token_pairs)
    d_out_weight = out_weight_grad(
        after(heads_all, token_pairs[2]), [grad_chunks[j] for j in range(4)]
    )
    ahead, behind = add_passed(token_pairs, passed)
    ahead, behind = after((ahead, behind), d_out_weight, *out_pieces)
    token_pieces = [from_ring(ahead, 3, False), from_ring(behind, 1, False)]
    d_qkv_weight = qkv_weight_grad(
        [chunks[j] for j in range(4)], after(projected_grads, ahead), local_heads
    )
    token_pieces.append(after(token_pairs[0], d_qkv_weight))
    output, d_tokens = scatter_near(out_pieces, token_pieces)
    d_out_weight = d_out_weight.reshape(local_heads, head_size, width_part)
    return (output, d_tokens, d_qkv_weight, d_out_weight)


def solution(mesh):
    in_specs = (
        P(("row", "col"), "depth"),
        P("depth", ("row", "col"), None, None),
        P(("row", "col"), None, "depth"),
        P("depth"),
        P(("row", "col"), "depth"),
    )
    out_specs = (
        P(("row", "col"), "depth"),
        P(("row", "col"), "depth"),
        P("depth", ("row", "col"), None, None),
        P(("row", "col"), None, "depth"),
    )
    return jax.shard_map(
        per_device, mesh=mesh, in_specs=in_specs, out_specs=out_specs, check_vma=False
    )
```

```python
import math

import jax
import jax.numpy as jnp
from jax import lax
from jax.experimental import pallas as pl
from jax.experimental.pallas import tpu as pltpu
from jax.sharding import PartitionSpec as P

PLANE = ("row", "col")
BLOCK = 32
BLOCKS = 32
OFFSETS = (1, 3, 2)
SENDS = (2, 1, 3, 0)
VMEM = pl.BlockSpec(memory_space=pltpu.VMEM)
NO_COST = pl.CostEstimate(flops=0, bytes_accessed=0, transcendentals=0)


def plane_index(x, y, core):
    return ((x % 2) * 2 + core) * 8 + (x // 2) * 4 + y


def ring_pairs(offset, first):
    pairs = []
    for x in range(4):
        for y in range(4):
            for core in range(2):
                along_x = (core == 0) == first
                sx, sy = ((x + offset) % 4, y) if along_x else (x, (y + offset) % 4)
                pairs.append((plane_index(sx, sy, core), plane_index(x, y, core)))
    return pairs


def core_pairs():
    return [
        (plane_index(x, y, core), plane_index(x, y, 1 - core))
        for x in range(4)
        for y in range(4)
        for core in range(2)
    ]


def depth_pairs(offset):
    return [((z + offset) % 4, z) for z in range(4)]


def swap_cores(rows):
    return lax.ppermute(rows, PLANE, core_pairs())


def from_ring(rows, offset, first):
    return lax.ppermute(rows, PLANE, ring_pairs(offset, first))


def from_depth(rows, offset):
    return lax.ppermute(rows, "depth", depth_pairs(offset))


def block_tables(depth):
    row, col = lax.axis_index("row"), lax.axis_index("col")
    x, y, core = (col // 4) * 2 + row // 2, col % 4, row % 2
    place = jnp.arange(BLOCKS, dtype=jnp.int32)
    j, family, i = place // 8, (place // 4) % 2, place % 4
    j = jnp.where(j >= 2, 5 - j, j)
    of_core = (core + family) % 2
    dx, dy = jnp.where(of_core == 0, i, j), jnp.where(of_core == 0, j, i)
    sx, sy = (x + dx) % 4, (y + dy) % 4
    sequence = (sx % 2) * 2 + of_core
    forward = ((sequence - depth + 4) % 4) * 8 + (sx // 2) * 4 + sy
    sequence = (place // 8 + depth) % 4
    of_core = sequence % 2
    sx, sy = ((place % 8) // 4) * 2 + sequence // 2, place % 4
    family = (of_core + core) % 2
    dx, dy = (sx - x + 4) % 4, (sy - y + 4) % 4
    i, j = jnp.where(of_core == 0, dx, dy), jnp.where(of_core == 0, dy, dx)
    inverse = family * 16 + jnp.where(j == 0, 3, jnp.where(j == 2, 0, (j + 1) // 2)) * 4 + i
    return forward.astype(jnp.int32), inverse.astype(jnp.int32)


def place_blocks(parts, table, outs=1):
    columns = parts[0].shape[-1]
    per_part, per_out = BLOCKS // len(parts), BLOCKS // outs
    parts = [part.reshape(-1, BLOCK, columns) for part in parts]

    def kernel(table_ref, *refs):
        *refs, placed = refs
        for at, ref in enumerate(refs[: len(parts)]):
            for b in range(per_part):
                placed[table_ref[at * per_part + b]] = ref[b]
        for k, ref in enumerate(refs[len(parts) :]):
            ref[...] = placed[k * per_out : (k + 1) * per_out]

    placed = pl.pallas_call(
        kernel,
        out_shape=(jax.ShapeDtypeStruct((per_out, BLOCK, columns), parts[0].dtype),) * outs,
        in_specs=[pl.BlockSpec(memory_space=pltpu.SMEM)] + [VMEM] * len(parts),
        out_specs=(VMEM,) * outs,
        scratch_shapes=[pltpu.VMEM((BLOCKS, BLOCK, columns), parts[0].dtype)],
        compiler_params=pltpu.CompilerParams(vmem_limit_bytes=24 * 2**20),
        cost_estimate=NO_COST,
    )(table, *parts)
    return [out.reshape(per_out * BLOCK, columns) for out in placed]


def softmax_rows(queries, key_rows, positions, score_scale):
    size = queries.shape[0]
    scores = lax.dot_general(
        queries, key_rows, (((1,), (1,)), ((), ())), preferred_element_type=jnp.float32
    )
    i = lax.broadcasted_iota(jnp.int32, (size, size), 0)
    j = lax.broadcasted_iota(jnp.int32, (size, size), 1)
    allowed = (j <= i) & (j >= i - positions)
    weights = jnp.where(allowed, jnp.exp(scores * score_scale), 0.0)
    return weights / jnp.sum(weights, axis=-1, keepdims=True)


def attend(parts, d_mixed, positions, heads, score_scale):
    seq_len, columns = parts[0].shape
    size = columns // (3 * heads)
    width = heads * size

    def kernel(p0, p1, p2, p3, d1, d2, d3, positions_ref, projected_ref, mixed_ref, *sends):
        projected_ref[...] = sum_float32([p0[...], p1[...], p2[...], p3[...]]).astype(jnp.bfloat16)
        for h in range(heads):
            q, k, v = (projected_ref[:, (h * 3 + c) * size : (h * 3 + c + 1) * size] for c in range(3))
            rounded = softmax_rows(q, k, positions_ref[...], score_scale).astype(jnp.bfloat16)
            mixed_ref[:, h * size : (h + 1) * size] = jnp.dot(
                rounded, v, preferred_element_type=jnp.float32
            ).astype(jnp.bfloat16)
        for d_mixed_ref, ref in zip((d1, d2, d3), sends):
            ref[:seq_len] = mixed_ref[...]
            ref[seq_len:] = d_mixed_ref[...]

    return pl.pallas_call(
        kernel,
        out_shape=(
            jax.ShapeDtypeStruct((seq_len, columns), jnp.bfloat16),
            jax.ShapeDtypeStruct((seq_len, width), jnp.bfloat16),
        )
        + (jax.ShapeDtypeStruct((2 * seq_len, width), jnp.bfloat16),) * 3,
        in_specs=[VMEM] * 8,
        out_specs=(VMEM,) * 5,
        compiler_params=pltpu.CompilerParams(vmem_limit_bytes=24 * 2**20),
        cost_estimate=NO_COST,
    )(*parts, *d_mixed[1:], positions.reshape(seq_len, 1))


def attend_back(projected, parts, positions, heads, score_scale):
    seq_len, columns = projected.shape
    size = columns // (3 * heads)

    def kernel(projected_ref, p0, p1, p2, p3, positions_ref, out_ref):
        d_mixed = sum_float32([p0[:seq_len]] + [p[seq_len:] for p in (p1, p2, p3)]).astype(jnp.bfloat16)
        contract_first = (((0,), (0,)), ((), ()))
        contract_last = (((1,), (1,)), ((), ()))
        for h in range(heads):
            q, k, v = (projected_ref[:, (h * 3 + c) * size : (h * 3 + c + 1) * size] for c in range(3))
            probabilities = softmax_rows(q, k, positions_ref[...], score_scale)
            rounded = probabilities.astype(jnp.bfloat16)
            grad = d_mixed[:, h * size : (h + 1) * size]
            d_probs = lax.dot_general(grad, v, contract_last, preferred_element_type=jnp.float32)
            row_delta = jnp.sum(probabilities * d_probs, axis=-1, keepdims=True)
            d_scores = (probabilities * (d_probs - row_delta) * score_scale).astype(jnp.bfloat16)
            grads = (
                jnp.dot(d_scores, k, preferred_element_type=jnp.float32),
                lax.dot_general(d_scores, q, contract_first, preferred_element_type=jnp.float32),
                lax.dot_general(rounded, grad, contract_first, preferred_element_type=jnp.float32),
            )
            for c in range(3):
                out_ref[:, (h * 3 + c) * size : (h * 3 + c + 1) * size] = grads[c].astype(jnp.bfloat16)

    return pl.pallas_call(
        kernel,
        out_shape=jax.ShapeDtypeStruct((seq_len, columns), jnp.bfloat16),
        in_specs=[VMEM] * 6,
        out_specs=VMEM,
        compiler_params=pltpu.CompilerParams(vmem_limit_bytes=24 * 2**20),
        cost_estimate=NO_COST,
    )(projected, *parts, positions.reshape(seq_len, 1))


def chunk_rows(ref, j):
    half = 4 * BLOCK
    at = SENDS.index(j) * half
    return jnp.concatenate([ref[at : at + half, :], ref[at + 4 * half : at + 5 * half, :]], axis=0)


def transposed_product(left, right):
    return lax.dot_general(
        left, right, (((0,), (0,)), ((), ())), preferred_element_type=jnp.float32
    )


def grad_cost(chunks, columns):
    rows, width = chunks[0].shape
    return pl.CostEstimate(
        flops=8 * rows * width * columns,
        bytes_accessed=8 * rows * (width + columns) + 4 * width * columns,
        transcendentals=0,
    )


def qkv_weight_grad(chunks, grads, heads):
    rows, width = chunks[0].shape
    columns = grads.shape[1]
    size = columns // (3 * heads)
    step = 512

    def kernel(c0, c1, c2, c3, grads_ref, out_ref):
        total = transposed_product(c0[...], chunk_rows(grads_ref, 0))
        for j, ref in enumerate((c1, c2, c3), 1):
            total = total + transposed_product(ref[...], chunk_rows(grads_ref, j))
        for h in range(heads):
            for c in range(3):
                at = (h * 3 + c) * size
                out_ref[pl.ds(c * heads + h, step, stride=3 * heads), :] = total[:, at : at + size]

    out = pl.pallas_call(
        kernel,
        grid=(width // step,),
        out_shape=jax.ShapeDtypeStruct((width * 3 * heads, size), jnp.float32),
        in_specs=[pl.BlockSpec((rows, step), lambda n: (0, n))] * 4
        + [pl.BlockSpec((4 * rows, columns), lambda n: (0, 0))],
        out_specs=pl.BlockSpec((step * 3 * heads, size), lambda n: (n, 0)),
        compiler_params=pltpu.CompilerParams(vmem_limit_bytes=24 * 2**20),
        cost_estimate=grad_cost(chunks, columns),
    )(*chunks, grads)
    return out.reshape(width, 3, heads, size).transpose(0, 2, 1, 3)


def out_weight_grad(mixed, chunks):
    rows, width = chunks[0].shape
    columns = mixed.shape[1]
    step = 512

    def kernel(mixed_ref, c0, c1, c2, c3, out_ref):
        total = transposed_product(chunk_rows(mixed_ref, 0), c0[...])
        for j, ref in enumerate((c1, c2, c3), 1):
            total = total + transposed_product(chunk_rows(mixed_ref, j), ref[...])
        out_ref[...] = total

    return pl.pallas_call(
        kernel,
        grid=(width // step,),
        out_shape=jax.ShapeDtypeStruct((columns, width), jnp.float32),
        in_specs=[pl.BlockSpec((4 * rows, columns), lambda n: (0, 0))]
        + [pl.BlockSpec((rows, step), lambda n: (0, n))] * 4,
        out_specs=pl.BlockSpec((columns, step), lambda n: (0, n)),
        compiler_params=pltpu.CompilerParams(vmem_limit_bytes=12 * 2**20),
        cost_estimate=grad_cost(chunks, columns),
    )(mixed, *chunks)


def after(value, *others):
    return lax.optimization_barrier((value,) + others)[0]


def sum_float32(parts):
    total = parts[0].astype(jnp.float32)
    for part in parts[1:]:
        total = total + part.astype(jnp.float32)
    return total


def pair_sums(own_term, others):
    return {j: sum_float32([own_term(j), others[j]]).astype(jnp.bfloat16) for j in SENDS}


def pass_on(pairs):
    half = pairs[2].shape[0] // 2
    return [from_ring(pairs[2][:half], 3, False), from_ring(pairs[2][half:], 1, False)]


def add_passed(pairs, passed):
    half = pairs[2].shape[0] // 2
    first = sum_float32([pairs[1][:half], passed[0]]).astype(jnp.bfloat16)
    last = sum_float32([pairs[3][half:], passed[1]]).astype(jnp.bfloat16)
    ahead = jnp.concatenate([first, pairs[1][half:]], axis=0)
    behind = jnp.concatenate([pairs[3][:half], last], axis=0)
    return ahead, behind


def scatter_near(*columns):
    sums = [sum_float32(pieces).astype(jnp.bfloat16) for pieces in columns]

    def part(i):
        return jnp.concatenate([rows[i * BLOCK : (i + 1) * BLOCK] for rows in sums], axis=0)

    parts = [part(0)] + [from_ring(part(i), 4 - i, True) for i in (2, 1, 3)]
    total = sum_float32(parts).astype(jnp.bfloat16)
    return [total[at * BLOCK : (at + 1) * BLOCK] for at in range(len(columns))]


def scatter_depth(blocks):
    return [blocks[0]] + [from_depth(blocks[k], 4 - k) for k in (1, 2, 3)]


def gather_depth(rows):
    ahead = {k: from_depth(rows, k) for k in (2, 1, 3)}
    return [rows, ahead[1], ahead[2], ahead[3]]


def per_device(tokens, w_qkv, w_out, positions, d_output):
    seq_len = positions.shape[0]
    local_heads = w_qkv.shape[1]
    head_size = w_qkv.shape[3]
    width_part = w_qkv.shape[0]
    score_scale = 1.0 / math.sqrt(head_size)
    out_flat = w_out.reshape(local_heads * head_size, width_part)
    contract_last = (((1,), (1,)), ((), ()))
    depth = lax.axis_index("depth")
    forward, inverse = block_tables(depth)

    near = {i: from_ring(tokens, i, True) for i in OFFSETS}
    near_grads = {i: from_ring(d_output, i, True) for i in (1, 3)}
    near[0] = tokens
    token_column = jnp.concatenate([near[i] for i in range(4)], axis=0)
    token_column = after(token_column, near_grads[1], near_grads[3])
    own = {j: from_ring(token_column, j, False) for j in OFFSETS}
    own[0] = token_column
    other = {0: swap_cores(token_column)}
    qkv_flat = after(w_qkv, token_column).reshape(width_part, local_heads * 3 * head_size).T
    near_grads[2] = from_ring(after(d_output, token_column), 2, True)
    near_grads[0] = d_output
    own[1], own[3] = after((own[1], own[3]), qkv_flat, other[0], near_grads[2])

    def product(chunk, weight):
        return lax.dot_general(
            chunk, weight, contract_last, preferred_element_type=jnp.float32
        ).astype(jnp.bfloat16)

    chunks = {0: jnp.concatenate([own[0], other[0]], axis=0)}
    grad_column = jnp.concatenate([near_grads[i] for i in range(4)], axis=0)
    other[1], other[3] = swap_cores(own[1]), swap_cores(own[3])
    own[2], grad_column = after((own[2], grad_column), other[1], other[3])
    other[2] = swap_cores(own[2])
    for j in OFFSETS:
        chunks[j] = jnp.concatenate([own[j], other[j]], axis=0)
    chunks[0] = after(chunks[0], own[2])
    parts = [product(chunks[j], qkv_flat) for j in (0, 1, 3, 2)]
    parts = place_blocks(parts, forward, 4)

    grad_column = after(grad_column, own[2])
    own_grads = {j: from_ring(grad_column, j, False) for j in (1, 3)}
    own_grads[0] = grad_column
    other_grads = {0: swap_cores(grad_column)}
    parts[1], parts[3] = after((parts[1], parts[3]), other_grads[0])
    parts[2] = after(parts[2], own_grads[1], own_grads[3])
    projected_parts = scatter_depth(parts)
    own_grads[2] = from_ring(after(grad_column, parts[0]), 2, False)
    own_grads[1], own_grads[3] = after((own_grads[1], own_grads[3]), own_grads[2])
    for j in (1, 3, 2):
        other_grads[j] = swap_cores(own_grads[j])
    grad_chunks = {
        j: jnp.concatenate([own_grads[j], other_grads[j]], axis=0) for j in range(4)
    }
    d_mixed = place_blocks(
        [product(grad_chunks[j], out_flat) for j in (0, 1, 3, 2)], forward, 4
    )

    projected, mixed, *sends = attend(
        projected_parts, d_mixed, positions, local_heads, score_scale
    )
    behind = [from_depth(sends[k - 1], 4 - k) for k in (1, 2, 3)]
    (heads_all,) = place_blocks([mixed] + behind[::-1], inverse)
    half = 4 * BLOCK
    out_others = jnp.dot(
        heads_all[4 * half :], out_flat, preferred_element_type=jnp.float32
    ).astype(jnp.bfloat16)
    d_projected = attend_back(
        after(projected, out_others), [d_mixed[0]] + behind, positions, local_heads, score_scale
    )

    out_others = swap_cores(after(out_others, d_projected))

    def out_term(j):
        at = SENDS.index(j) * half
        return jnp.dot(
            heads_all[at : at + half], out_flat, preferred_element_type=jnp.float32
        ).astype(jnp.bfloat16)

    out_pairs = pair_sums(
        out_term,
        {j: out_others[SENDS.index(j) * half : (SENDS.index(j) + 1) * half] for j in SENDS},
    )
    passed = pass_on(out_pairs)
    grad_parts = gather_depth(d_projected)
    ahead, behind = add_passed(out_pairs, passed)
    grad_parts[2], ahead, behind = after((grad_parts[2], ahead, behind))
    (projected_grads,) = place_blocks(grad_parts, inverse)
    out_pieces = [out_pairs[0], from_ring(ahead, 3, False), from_ring(behind, 1, False)]

    def token_term(start, rows):
        return jnp.dot(
            projected_grads[start : start + rows], qkv_flat, preferred_element_type=jnp.float32
        ).astype(jnp.bfloat16)

    first = token_term(4 * half, half)
    projected_grads = after(projected_grads, first)
    first = swap_cores(first)
    second = swap_cores(token_term(5 * half, 3 * half))
    token_pairs = pair_sums(
        lambda j: token_term(SENDS.index(j) * half, half),
        {2: first, 1: second[:half], 3: second[half : 2 * half], 0: second[2 * half :]},
    )
    passed = pass_on(token_pairs)
    d_out_weight = out_weight_grad(
        after(heads_all, token_pairs[2]), [grad_chunks[j] for j in range(4)]
    )
    ahead, behind = add_passed(token_pairs, passed)
    ahead, behind = after((ahead, behind), d_out_weight, *out_pieces)
    token_pieces = [from_ring(ahead, 3, False), from_ring(behind, 1, False)]
    d_qkv_weight = qkv_weight_grad(
        [chunks[j] for j in range(4)], after(projected_grads, ahead), local_heads
    )
    token_pieces.append(after(token_pairs[0], d_qkv_weight))
    output, d_tokens = scatter_near(out_pieces, token_pieces)
    d_out_weight = d_out_weight.reshape(local_heads, head_size, width_part)
    return (output, d_tokens, d_qkv_weight, d_out_weight)


def solution(mesh):
    in_specs = (
        P(("row", "col"), "depth"),
        P("depth", ("row", "col"), None, None),
        P(("row", "col"), None, "depth"),
        P("depth"),
        P(("row", "col"), "depth"),
    )
    out_specs = (
        P(("row", "col"), "depth"),
        P(("row", "col"), "depth"),
        P("depth", ("row", "col"), None, None),
        P(("row", "col"), None, "depth"),
    )
    return jax.shard_map(
        per_device, mesh=mesh, in_specs=in_specs, out_specs=out_specs, check_vma=False
    )
```

```python
import math

import jax
import jax.numpy as jnp
from jax import lax
from jax.experimental import pallas as pl
from jax.experimental.pallas import tpu as pltpu
from jax.sharding import PartitionSpec as P

PLANE = ("row", "col")
BLOCK = 32
BLOCKS = 32
OFFSETS = (1, 3, 2)
SENDS = (2, 1, 3, 0)
VMEM = pl.BlockSpec(memory_space=pltpu.VMEM)
NO_COST = pl.CostEstimate(flops=0, bytes_accessed=0, transcendentals=0)


def plane_index(x, y, core):
    return ((x % 2) * 2 + core) * 8 + (x // 2) * 4 + y


def ring_pairs(offset, first):
    pairs = []
    for x in range(4):
        for y in range(4):
            for core in range(2):
                along_x = (core == 0) == first
                sx, sy = ((x + offset) % 4, y) if along_x else (x, (y + offset) % 4)
                pairs.append((plane_index(sx, sy, core), plane_index(x, y, core)))
    return pairs


def core_pairs():
    return [
        (plane_index(x, y, core), plane_index(x, y, 1 - core))
        for x in range(4)
        for y in range(4)
        for core in range(2)
    ]


def depth_pairs(offset):
    return [((z + offset) % 4, z) for z in range(4)]


def swap_cores(rows):
    return lax.ppermute(rows, PLANE, core_pairs())


def from_ring(rows, offset, first):
    return lax.ppermute(rows, PLANE, ring_pairs(offset, first))


def from_depth(rows, offset):
    return lax.ppermute(rows, "depth", depth_pairs(offset))


def block_tables(depth):
    row, col = lax.axis_index("row"), lax.axis_index("col")
    x, y, core = (col // 4) * 2 + row // 2, col % 4, row % 2
    place = jnp.arange(BLOCKS, dtype=jnp.int32)
    j, family, i = place // 8, (place // 4) % 2, place % 4
    j = jnp.where(j >= 2, 5 - j, j)
    of_core = (core + family) % 2
    dx, dy = jnp.where(of_core == 0, i, j), jnp.where(of_core == 0, j, i)
    sx, sy = (x + dx) % 4, (y + dy) % 4
    sequence = (sx % 2) * 2 + of_core
    forward = ((sequence - depth + 4) % 4) * 8 + (sx // 2) * 4 + sy
    sequence = (place // 8 + depth) % 4
    of_core = sequence % 2
    sx, sy = ((place % 8) // 4) * 2 + sequence // 2, place % 4
    family = (of_core + core) % 2
    dx, dy = (sx - x + 4) % 4, (sy - y + 4) % 4
    i, j = jnp.where(of_core == 0, dx, dy), jnp.where(of_core == 0, dy, dx)
    inverse = family * 16 + jnp.where(j == 0, 3, jnp.where(j == 2, 0, (j + 1) // 2)) * 4 + i
    return forward.astype(jnp.int32), inverse.astype(jnp.int32)


def place_blocks(parts, table, outs=1):
    columns = parts[0].shape[-1]
    per_part, per_out = BLOCKS // len(parts), BLOCKS // outs
    parts = [part.reshape(-1, BLOCK, columns) for part in parts]

    def kernel(table_ref, *refs):
        *refs, placed = refs
        for at, ref in enumerate(refs[: len(parts)]):
            for b in range(per_part):
                placed[table_ref[at * per_part + b]] = ref[b]
        for k, ref in enumerate(refs[len(parts) :]):
            ref[...] = placed[k * per_out : (k + 1) * per_out]

    placed = pl.pallas_call(
        kernel,
        out_shape=(jax.ShapeDtypeStruct((per_out, BLOCK, columns), parts[0].dtype),) * outs,
        in_specs=[pl.BlockSpec(memory_space=pltpu.SMEM)] + [VMEM] * len(parts),
        out_specs=(VMEM,) * outs,
        scratch_shapes=[pltpu.VMEM((BLOCKS, BLOCK, columns), parts[0].dtype)],
        compiler_params=pltpu.CompilerParams(vmem_limit_bytes=24 * 2**20),
        cost_estimate=NO_COST,
    )(table, *parts)
    return [out.reshape(per_out * BLOCK, columns) for out in placed]


def softmax_rows(queries, key_rows, positions, score_scale):
    size = queries.shape[0]
    scores = lax.dot_general(
        queries, key_rows, (((1,), (1,)), ((), ())), preferred_element_type=jnp.float32
    )
    i = lax.broadcasted_iota(jnp.int32, (size, size), 0)
    j = lax.broadcasted_iota(jnp.int32, (size, size), 1)
    allowed = (j <= i) & (j >= i - positions)
    weights = jnp.where(allowed, jnp.exp(scores * score_scale), 0.0)
    return weights / jnp.sum(weights, axis=-1, keepdims=True)


def attend(parts, d_mixed, positions, heads, score_scale):
    seq_len, columns = parts[0].shape
    size = columns // (3 * heads)
    width = heads * size

    def kernel(p0, p1, p2, p3, d1, d2, d3, positions_ref, projected_ref, mixed_ref, *sends):
        projected_ref[...] = sum_float32([p0[...], p1[...], p2[...], p3[...]]).astype(jnp.bfloat16)
        for h in range(heads):
            q, k, v = (projected_ref[:, (h * 3 + c) * size : (h * 3 + c + 1) * size] for c in range(3))
            rounded = softmax_rows(q, k, positions_ref[...], score_scale).astype(jnp.bfloat16)
            mixed_ref[:, h * size : (h + 1) * size] = jnp.dot(
                rounded, v, preferred_element_type=jnp.float32
            ).astype(jnp.bfloat16)
        for d_mixed_ref, ref in zip((d1, d2, d3), sends):
            ref[:seq_len] = mixed_ref[...]
            ref[seq_len:] = d_mixed_ref[...]

    return pl.pallas_call(
        kernel,
        out_shape=(
            jax.ShapeDtypeStruct((seq_len, columns), jnp.bfloat16),
            jax.ShapeDtypeStruct((seq_len, width), jnp.bfloat16),
        )
        + (jax.ShapeDtypeStruct((2 * seq_len, width), jnp.bfloat16),) * 3,
        in_specs=[VMEM] * 8,
        out_specs=(VMEM,) * 5,
        compiler_params=pltpu.CompilerParams(vmem_limit_bytes=24 * 2**20),
        cost_estimate=NO_COST,
    )(*parts, *d_mixed[1:], positions.reshape(seq_len, 1))


def attend_back(projected, parts, positions, heads, score_scale):
    seq_len, columns = projected.shape
    size = columns // (3 * heads)

    def kernel(projected_ref, p0, p1, p2, p3, positions_ref, out_ref):
        d_mixed = sum_float32([p0[:seq_len]] + [p[seq_len:] for p in (p1, p2, p3)]).astype(jnp.bfloat16)
        contract_first = (((0,), (0,)), ((), ()))
        contract_last = (((1,), (1,)), ((), ()))
        for h in range(heads):
            q, k, v = (projected_ref[:, (h * 3 + c) * size : (h * 3 + c + 1) * size] for c in range(3))
            probabilities = softmax_rows(q, k, positions_ref[...], score_scale)
            rounded = probabilities.astype(jnp.bfloat16)
            grad = d_mixed[:, h * size : (h + 1) * size]
            d_probs = lax.dot_general(grad, v, contract_last, preferred_element_type=jnp.float32)
            row_delta = jnp.sum(probabilities * d_probs, axis=-1, keepdims=True)
            d_scores = (probabilities * (d_probs - row_delta) * score_scale).astype(jnp.bfloat16)
            grads = (
                jnp.dot(d_scores, k, preferred_element_type=jnp.float32),
                lax.dot_general(d_scores, q, contract_first, preferred_element_type=jnp.float32),
                lax.dot_general(rounded, grad, contract_first, preferred_element_type=jnp.float32),
            )
            for c in range(3):
                out_ref[:, (h * 3 + c) * size : (h * 3 + c + 1) * size] = grads[c].astype(jnp.bfloat16)

    return pl.pallas_call(
        kernel,
        out_shape=jax.ShapeDtypeStruct((seq_len, columns), jnp.bfloat16),
        in_specs=[VMEM] * 6,
        out_specs=VMEM,
        compiler_params=pltpu.CompilerParams(vmem_limit_bytes=24 * 2**20),
        cost_estimate=NO_COST,
    )(projected, *parts, positions.reshape(seq_len, 1))


def chunk_rows(ref, j):
    half = 4 * BLOCK
    at = SENDS.index(j) * half
    return jnp.concatenate([ref[at : at + half, :], ref[at + 4 * half : at + 5 * half, :]], axis=0)


def transposed_product(left, right):
    return lax.dot_general(
        left, right, (((0,), (0,)), ((), ())), preferred_element_type=jnp.float32
    )


def grad_cost(chunks, columns):
    rows, width = chunks[0].shape
    return pl.CostEstimate(
        flops=8 * rows * width * columns,
        bytes_accessed=8 * rows * (width + columns) + 4 * width * columns,
        transcendentals=0,
    )


def qkv_weight_grad(chunks, grads, heads):
    rows, width = chunks[0].shape
    columns = grads.shape[1]
    size = columns // (3 * heads)
    step = 512

    def kernel(c0, c1, c2, c3, grads_ref, out_ref):
        total = transposed_product(c0[...], chunk_rows(grads_ref, 0))
        for j, ref in enumerate((c1, c2, c3), 1):
            total = total + transposed_product(ref[...], chunk_rows(grads_ref, j))
        for h in range(heads):
            for c in range(3):
                at = (h * 3 + c) * size
                out_ref[pl.ds(c * heads + h, step, stride=3 * heads), :] = total[:, at : at + size]

    out = pl.pallas_call(
        kernel,
        grid=(width // step,),
        out_shape=jax.ShapeDtypeStruct((width * 3 * heads, size), jnp.float32),
        in_specs=[pl.BlockSpec((rows, step), lambda n: (0, n))] * 4
        + [pl.BlockSpec((4 * rows, columns), lambda n: (0, 0))],
        out_specs=pl.BlockSpec((step * 3 * heads, size), lambda n: (n, 0)),
        compiler_params=pltpu.CompilerParams(vmem_limit_bytes=24 * 2**20),
        cost_estimate=grad_cost(chunks, columns),
    )(*chunks, grads)
    return out.reshape(width, 3, heads, size).transpose(0, 2, 1, 3)


def out_weight_grad(mixed, chunks):
    rows, width = chunks[0].shape
    columns = mixed.shape[1]
    step = 512

    def kernel(mixed_ref, c0, c1, c2, c3, out_ref):
        total = transposed_product(chunk_rows(mixed_ref, 0), c0[...])
        for j, ref in enumerate((c1, c2, c3), 1):
            total = total + transposed_product(chunk_rows(mixed_ref, j), ref[...])
        out_ref[...] = total

    return pl.pallas_call(
        kernel,
        grid=(width // step,),
        out_shape=jax.ShapeDtypeStruct((columns, width), jnp.float32),
        in_specs=[pl.BlockSpec((4 * rows, columns), lambda n: (0, 0))]
        + [pl.BlockSpec((rows, step), lambda n: (0, n))] * 4,
        out_specs=pl.BlockSpec((columns, step), lambda n: (0, n)),
        compiler_params=pltpu.CompilerParams(vmem_limit_bytes=12 * 2**20),
        cost_estimate=grad_cost(chunks, columns),
    )(mixed, *chunks)


def after(value, *others):
    return lax.optimization_barrier((value,) + others)[0]


def sum_float32(parts):
    total = parts[0].astype(jnp.float32)
    for part in parts[1:]:
        total = total + part.astype(jnp.float32)
    return total


def pair_sums(own_term, others):
    return {j: sum_float32([own_term(j), others[j]]).astype(jnp.bfloat16) for j in SENDS}


def pass_on(pairs):
    half = pairs[2].shape[0] // 2
    return [from_ring(pairs[2][:half], 3, False), from_ring(pairs[2][half:], 1, False)]


def add_passed(pairs, passed):
    half = pairs[2].shape[0] // 2
    first = sum_float32([pairs[1][:half], passed[0]]).astype(jnp.bfloat16)
    last = sum_float32([pairs[3][half:], passed[1]]).astype(jnp.bfloat16)
    ahead = jnp.concatenate([first, pairs[1][half:]], axis=0)
    behind = jnp.concatenate([pairs[3][:half], last], axis=0)
    return ahead, behind


def scatter_near(*columns):
    sums = [sum_float32(pieces).astype(jnp.bfloat16) for pieces in columns]

    def part(i):
        return jnp.concatenate([rows[i * BLOCK : (i + 1) * BLOCK] for rows in sums], axis=0)

    parts = [part(0)] + [from_ring(part(i), 4 - i, True) for i in (2, 1, 3)]
    total = sum_float32(parts).astype(jnp.bfloat16)
    return [total[at * BLOCK : (at + 1) * BLOCK] for at in range(len(columns))]


def scatter_depth(blocks):
    return [blocks[0]] + [from_depth(blocks[k], 4 - k) for k in (1, 2, 3)]


def gather_depth(rows):
    ahead = {k: from_depth(rows, k) for k in (2, 1, 3)}
    return [rows, ahead[1], ahead[2], ahead[3]]


def per_device(tokens, w_qkv, w_out, positions, d_output):
    seq_len = positions.shape[0]
    local_heads = w_qkv.shape[1]
    head_size = w_qkv.shape[3]
    width_part = w_qkv.shape[0]
    score_scale = 1.0 / math.sqrt(head_size)
    out_flat = w_out.reshape(local_heads * head_size, width_part)
    contract_last = (((1,), (1,)), ((), ()))
    depth = lax.axis_index("depth")
    forward, inverse = block_tables(depth)

    near = {i: from_ring(tokens, i, True) for i in OFFSETS}
    near_grads = {i: from_ring(d_output, i, True) for i in (1, 3)}
    near[0] = tokens
    token_column = jnp.concatenate([near[i] for i in range(4)], axis=0)
    token_column = after(token_column, near_grads[1], near_grads[3])
    own = {j: from_ring(token_column, j, False) for j in OFFSETS}
    own[0] = token_column
    other = {0: swap_cores(token_column)}
    qkv_flat = after(w_qkv, token_column).reshape(width_part, local_heads * 3 * head_size).T
    near_grads[2] = from_ring(after(d_output, token_column), 2, True)
    near_grads[0] = d_output
    own[1], own[3] = after((own[1], own[3]), qkv_flat, other[0], near_grads[2])

    def product(chunk, weight):
        return lax.dot_general(
            chunk, weight, contract_last, preferred_element_type=jnp.float32
        ).astype(jnp.bfloat16)

    chunks = {0: jnp.concatenate([own[0], other[0]], axis=0)}
    grad_column = jnp.concatenate([near_grads[i] for i in range(4)], axis=0)
    other[1], other[3] = swap_cores(own[1]), swap_cores(own[3])
    own[2], grad_column = after((own[2], grad_column), other[1], other[3])
    other[2] = swap_cores(own[2])
    for j in OFFSETS:
        chunks[j] = jnp.concatenate([own[j], other[j]], axis=0)
    chunks[0] = after(chunks[0], own[2])
    parts = [product(chunks[j], qkv_flat) for j in (0, 1, 3, 2)]
    parts = place_blocks(parts, forward, 4)

    grad_column = after(grad_column, own[2])
    own_grads = {j: from_ring(grad_column, j, False) for j in (1, 3)}
    own_grads[0] = grad_column
    other_grads = {0: swap_cores(grad_column)}
    parts[1], parts[3] = after((parts[1], parts[3]), other_grads[0])
    parts[2] = after(parts[2], own_grads[1], own_grads[3])
    projected_parts = scatter_depth(parts)
    own_grads[2] = from_ring(after(grad_column, parts[0]), 2, False)
    own_grads[1], own_grads[3] = after((own_grads[1], own_grads[3]), own_grads[2])
    for j in (1, 3, 2):
        other_grads[j] = swap_cores(own_grads[j])
    grad_chunks = {
        j: jnp.concatenate([own_grads[j], other_grads[j]], axis=0) for j in range(4)
    }
    d_mixed = place_blocks(
        [product(grad_chunks[j], out_flat) for j in (0, 1, 3, 2)], forward, 4
    )

    projected, mixed, *sends = attend(
        projected_parts, d_mixed, positions, local_heads, score_scale
    )
    behind = [from_depth(sends[k - 1], 4 - k) for k in (1, 2, 3)]
    d_projected = attend_back(
        projected, [d_mixed[0]] + behind, positions, local_heads, score_scale
    )
    (heads_all,) = place_blocks(after([mixed] + behind[::-1], d_projected), inverse)
    half = 4 * BLOCK
    out_others = jnp.dot(
        heads_all[4 * half :], out_flat, preferred_element_type=jnp.float32
    ).astype(jnp.bfloat16)
    out_others = swap_cores(out_others)

    def out_term(j):
        at = SENDS.index(j) * half
        return jnp.dot(
            heads_all[at : at + half], out_flat, preferred_element_type=jnp.float32
        ).astype(jnp.bfloat16)

    out_pairs = pair_sums(
        out_term,
        {j: out_others[SENDS.index(j) * half : (SENDS.index(j) + 1) * half] for j in SENDS},
    )
    passed = pass_on(out_pairs)
    grad_parts = gather_depth(d_projected)
    ahead, behind = add_passed(out_pairs, passed)
    grad_parts[2], ahead, behind = after((grad_parts[2], ahead, behind))
    (projected_grads,) = place_blocks(grad_parts, inverse)
    out_pieces = [out_pairs[0], from_ring(ahead, 3, False), from_ring(behind, 1, False)]

    def token_term(start, rows):
        return jnp.dot(
            projected_grads[start : start + rows], qkv_flat, preferred_element_type=jnp.float32
        ).astype(jnp.bfloat16)

    first = token_term(4 * half, half)
    projected_grads = after(projected_grads, first)
    first = swap_cores(first)
    second = swap_cores(token_term(5 * half, 3 * half))
    token_pairs = pair_sums(
        lambda j: token_term(SENDS.index(j) * half, half),
        {2: first, 1: second[:half], 3: second[half : 2 * half], 0: second[2 * half :]},
    )
    passed = pass_on(token_pairs)
    d_out_weight = out_weight_grad(
        after(heads_all, token_pairs[2]), [grad_chunks[j] for j in range(4)]
    )
    ahead, behind = add_passed(token_pairs, passed)
    ahead, behind = after((ahead, behind), d_out_weight, *out_pieces)
    token_pieces = [from_ring(ahead, 3, False), from_ring(behind, 1, False)]
    d_qkv_weight = qkv_weight_grad(
        [chunks[j] for j in range(4)], after(projected_grads, ahead), local_heads
    )
    token_pieces.append(after(token_pairs[0], d_qkv_weight))
    output, d_tokens = scatter_near(out_pieces, token_pieces)
    d_out_weight = d_out_weight.reshape(local_heads, head_size, width_part)
    return (output, d_tokens, d_qkv_weight, d_out_weight)


def solution(mesh):
    in_specs = (
        P(("row", "col"), "depth"),
        P("depth", ("row", "col"), None, None),
        P(("row", "col"), None, "depth"),
        P("depth"),
        P(("row", "col"), "depth"),
    )
    out_specs = (
        P(("row", "col"), "depth"),
        P(("row", "col"), "depth"),
        P("depth", ("row", "col"), None, None),
        P(("row", "col"), None, "depth"),
    )
    return jax.shard_map(
        per_device, mesh=mesh, in_specs=in_specs, out_specs=out_specs, check_vma=False
    )
```
